256 devices in a mesh: seq: 64 (over x, y, z_lo, core), head: 4 (over z_hi).
Axes of the slice: x: 4, y: 4, z: 8 (z_hi: 4, z_lo: 2; z = z_hi * 2 + z_lo), core: 2. Of those that a mesh axis runs over, the one named last changes fastest.
Arguments:
- queries: bfloat16 [32768, 2048], P('seq', 'head'), may hold values from -7.5 to 7.5
- key_rows: bfloat16 [32768, 2048], P('seq', 'head'), may hold values from -7.5 to 7.5
- value_rows: bfloat16 [32768, 4096], P('seq', 'head'), may hold values from -6 to 6
- input_gate: float32 [32768, 8], P('seq', 'head'), may hold values from -3 to 220
- forget_gate: float32 [32768, 8], P('seq', 'head')
- out_weight: bfloat16 [4096, 4096], P('head', 'seq'), may hold values from -0.25 to 0.25
Outputs:
- projected: bfloat16 [32768, 4096], P('seq', 'head')
The draws below stay inside these ranges and needn't reach their ends.
All inputs are finite; a program needn't handle non-finite values.
Results may differ from the reference program's by a relative error of at most 0.015.
Values may be sent and summed in bfloat16 or wider, within the bound.
No kernel may reach another device: no remote copies, remote signals or barrier semaphores. Data moves between devices by JAX's collectives and lax.ppermute only.
A program may use at most 192 MiB of HBM per device.

```python
import jax
import jax.numpy as jnp
from jax import lax

D = 4096
H = 8
DH = 512
DK = 256
T_DEV = 512
TOKENS = 32768


def shared_direction(key):
    common = jax.random.normal(jax.random.fold_in(key, 101), (H * DK,), jnp.float32)
    return 0.5 * jnp.clip(common, -3.0, 3.0)


def fast_heads(key, share):
    chance = jax.random.uniform(jax.random.fold_in(key, 201), (H,), jnp.float32)
    forced = jax.random.randint(jax.random.fold_in(key, 202), (), 0, H)
    return (chance < share) | (jnp.arange(H) == forced)


def noisy_rows(key):
    noise = jnp.clip(jax.random.normal(key, (TOKENS, H * DK), jnp.float32), -6.0, 6.0)
    return noise


def draw_queries(key, part):
    common = shared_direction(key)
    key = jax.random.fold_in(key, 3)
    return (noisy_rows(key) + common[None, :]).astype(jnp.bfloat16)


def draw_key_rows(key, part):
    common = shared_direction(key)
    key = jax.random.fold_in(key, 5)
    return (noisy_rows(key) + common[None, :]).astype(jnp.bfloat16)


def draw_input_gate(key, part):
    share = 0.5
    quick = fast_heads(key, share)
    key = jax.random.fold_in(key, 7)
    first = jax.random.fold_in(key, 0)
    fourth = jax.random.fold_in(key, 3)
    fifth = jax.random.fold_in(key, 4)
    values = jax.random.uniform(first, (TOKENS, H), jnp.float32, -3.0, 3.0)
    shard_positions = jnp.arange(TOKENS)[:, None, None]
    token_positions = jax.random.randint(fourth, (3, H), 0, TOKENS)
    height = 16.0 + 8.0 * jax.random.uniform(fifth, (3, H), jnp.float32)
    raised = jnp.max(jnp.where(shard_positions == token_positions[None], height[None], -1000.0), axis=1)
    raised = jnp.where(quick[None, :], raised, -1000.0)
    values = jnp.maximum(values, raised)
    return values.astype(jnp.float32)


def draw_forget_gate(key, part):
    share = 0.5
    quick = fast_heads(key, share)
    key = jax.random.fold_in(key, 11)
    keys_list = jax.random.split(key, 4)
    rate = jnp.where(quick, 1.0 / 40.0, 0.3 / TOKENS)
    token_multiplier = jnp.exp(jax.random.uniform(keys_list[1], (TOKENS, H), jnp.float32, -0.7, 0.7))
    block_factor = jnp.exp(jax.random.uniform(keys_list[2], (TOKENS // T_DEV, H), jnp.float32, -0.7, 0.7))
    block_factor = jnp.repeat(block_factor, T_DEV, axis=0)
    forget_log_gate = -rate[None, :] * token_multiplier * block_factor
    token_positions = jax.random.randint(keys_list[3], (4, H), 0, TOKENS)
    shard_positions = jnp.arange(TOKENS)[:, None, None]
    token_span = jnp.any(shard_positions == token_positions[None], axis=1)
    forget_log_gate = jnp.where(token_span, jnp.log(0.7), forget_log_gate)
    return (forget_log_gate - jnp.log(-jnp.expm1(forget_log_gate))).astype(jnp.float32)


def spiked(array, stream_key, source, target, shards_of, factor):
    def block_of(axis_at):
        return (jnp.arange(array.shape[axis_at]) // (array.shape[axis_at] // shards_of)).reshape((-1,) + (1,) * (array.ndim - 1 - axis_at))

    one_side = jax.random.permutation(stream_key, shards_of)[block_of(target)]
    second = (block_of(target) + shards_of // 2) % shards_of
    return jnp.where((block_of(source) == one_side) | (block_of(source) == second), factor * array, array)


def shard_levels(key, shape, shards, smallest, high):
    def one(axis_at, blocks):
        draws = jax.random.uniform(jax.random.fold_in(jax.random.fold_in(key, 6), axis_at), (blocks,), jnp.float32, smallest / len(shards), high / len(shards))
        return jnp.repeat(jnp.exp(draws), shape[axis_at] // blocks).reshape((-1,) + (1,) * (len(shape) - axis_at - 1))

    level = one(*shards[0])
    for cut in shards[1:]:
        level = level * one(*cut)
    return level


def gaussian(rng, extent, width, bound, cuts=(), held_as=jnp.bfloat16):
    entries = jax.random.normal(rng, extent, jnp.float32) * width
    if len(cuts) > 0:
        entries = shard_levels(rng, extent, cuts, -0.22, 0.18) * entries
    return jnp.clip(entries, min=-bound, max=bound).astype(held_as)


def heavy_noise(stream_key, extent, deviation, bound, cuts, heavy, dtype=jnp.bfloat16):
    values = deviation * jax.random.normal(stream_key, extent, jnp.float32)
    if cuts:
        values = values * shard_levels(stream_key, extent, cuts, -0.22, 0.18)
    return jnp.clip(spiked(values, jax.random.fold_in(stream_key, 3), *heavy), -bound, bound).astype(dtype)


def setup_inputs(seed: int = 0) -> dict:
    key_list = jax.random.split(jax.random.key(seed), 7)
    return {
        "queries": draw_queries(jax.random.fold_in(key_list[6], 71), 0),
        "key_rows": draw_key_rows(jax.random.fold_in(key_list[6], 71), 0),
        "value_rows": gaussian(key_list[2], (TOKENS, D), 1.0, 6.0, ((0, 64), (1, 4))),
        "input_gate": draw_input_gate(jax.random.fold_in(key_list[6], 71), 0),
        "forget_gate": draw_forget_gate(jax.random.fold_in(key_list[6], 71), 0),
        "out_weight": heavy_noise(key_list[5], (D, D), D ** -0.5, 0.25, ((0, 4), (1, 64)), (0, 1, 64, 4.0)),
    }


def local_terms(queries, key_rows, value_rows, in_gate, forget):
    score_scale = DK ** -0.5
    highest = lax.Precision.HIGHEST
    decay_sum = jnp.cumsum(jax.nn.log_sigmoid(forget), axis=0)
    scores = jnp.einsum("thd,jhd->htj", queries.astype(jnp.float32), key_rows.astype(jnp.float32), precision=highest) * score_scale
    length = queries.shape[0]
    causal = jnp.arange(length)[:, None] >= jnp.arange(length)[None, :]
    weight_logits = decay_sum.T[:, :, None] - decay_sum.T[:, None, :] + in_gate.T[:, None, :]
    weight_logits = jnp.where(causal[None], weight_logits, -jnp.inf)
    row_peak = jnp.max(weight_logits, axis=2)
    weights = (jnp.exp(weight_logits - row_peak[:, :, None]) * scores).astype(jnp.bfloat16)
    intra_numer = jnp.einsum("htj,jhd->thd", weights.astype(jnp.float32), value_rows.astype(jnp.float32), precision=highest)
    intra_denom = jnp.sum(weights.astype(jnp.float32), axis=2).T
    shard_decay = decay_sum[-1]
    log_source = shard_decay[None, :] - decay_sum + in_gate
    local_peak = jnp.max(log_source, axis=0)
    scaled_keys = key_rows.astype(jnp.float32) * jnp.exp(log_source - local_peak[None, :])[:, :, None]
    local_normal = jnp.sum(scaled_keys, axis=0)
    weighted_keys = scaled_keys.astype(jnp.bfloat16)
    local_memory = jnp.einsum("jhd,jhe->hde", weighted_keys.astype(jnp.float32), value_rows.astype(jnp.float32), precision=highest)
    return (intra_numer, intra_denom, row_peak.T, decay_sum), (shard_decay, local_memory, local_normal, local_peak)


def combine(earlier, latter):
    running_maximum = jnp.maximum(earlier[3] + latter[0], latter[3])
    prior_scale = jnp.exp(earlier[3] + latter[0] - running_maximum)
    local_scale = jnp.exp(latter[3] - running_maximum)
    memory = earlier[1] * prior_scale[:, None, None] + latter[1] * local_scale[:, None, None]
    normal = earlier[2] * prior_scale[:, None] + latter[2] * local_scale[:, None]
    return (earlier[0] + latter[0], memory, normal, running_maximum)


def readout(queries, pieces, carried):
    intra_numer, intra_denom, row_peak, decay_sum = pieces
    highest = lax.Precision.HIGHEST
    score_scale = DK ** -0.5
    prior = decay_sum + carried[3][None, :]
    running_maximum = jnp.maximum(prior, row_peak)
    prior_scale = jnp.exp(prior - running_maximum)
    local_scale = jnp.exp(row_peak - running_maximum)
    query_float = queries.astype(jnp.float32)
    memory_read = carried[1].astype(jnp.bfloat16).astype(jnp.float32)
    from_memory = jnp.einsum("thd,hde->the", query_float, memory_read, precision=highest) * score_scale
    from_normal = jnp.einsum("thd,hd->th", query_float, carried[2], precision=highest) * score_scale
    numerator = prior_scale[:, :, None] * from_memory + local_scale[:, :, None] * intra_numer
    denominator = prior_scale * from_normal + local_scale * intra_denom
    floor_value = jnp.maximum(jnp.abs(denominator), 1.0)
    return (numerator / floor_value[:, :, None]).astype(jnp.bfloat16)


def reference(queries, key_rows, value_rows, input_gate, forget_gate, out_weight):
    blocks = TOKENS // T_DEV
    query_blocks = queries.reshape(blocks, T_DEV, H, DK)
    key_blocks = key_rows.reshape(blocks, T_DEV, H, DK)
    value_blocks = value_rows.reshape(blocks, T_DEV, H, DH)
    input_blocks = input_gate.reshape(blocks, T_DEV, H)
    forget_blocks = forget_gate.reshape(blocks, T_DEV, H)
    start = (jnp.zeros((H,), jnp.float32), jnp.zeros((H, DK, DH), jnp.float32), jnp.zeros((H, DK), jnp.float32), jnp.zeros((H,), jnp.float32))

    def advance(carried, block):
        pieces, summary = local_terms(block[0], block[1], block[2], block[3], block[4])
        hidden = readout(block[0], pieces, carried)
        return combine(carried, summary), hidden

    unused, hidden = lax.scan(advance, start, (query_blocks, key_blocks, value_blocks, input_blocks, forget_blocks))
    hidden = hidden.reshape(TOKENS, D)
    return jnp.dot(hidden, out_weight, preferred_element_type=jnp.float32).astype(jnp.bfloat16)
```

```python
import jax
import jax.numpy as jnp
from jax import lax
from jax.experimental import pallas as pl
from jax.experimental.pallas import tpu as pltpu
from jax.sharding import Mesh, PartitionSpec as P

DH = 512
DK = 256
T = 512
BLOCKS = 64
SLICE = 8
EXT = DH + 128
SEQ = ("x", "y", "z", "c")
CHUNKS = 4
F32 = jnp.float32
BF16 = jnp.bfloat16
SCALE = DK ** (-0.5)
LOWEST = -1e30
HBM = pltpu.MemorySpace.HBM


def split3(a):
    hi = a.astype(BF16).astype(F32)
    rest = a - hi
    mid = rest.astype(BF16).astype(F32)
    return hi, mid, rest - mid


def lanes(shape):
    return lax.broadcasted_iota(jnp.int32, shape, len(shape) - 1)


def rows(shape):
    return lax.broadcasted_iota(jnp.int32, shape, 0)


def place(columns, shape):
    lane = lanes(shape)
    out = jnp.zeros(shape, F32)
    for i, column in enumerate(columns):
        out = jnp.where(lane == i, column, out)
    return out


def pick(tile, first, count):
    lane = lanes(tile.shape)
    keep = (lane >= first) & (lane < first + count)
    return jnp.sum(jnp.where(keep, tile, 0.0), axis=1, keepdims=True)


def running_sum(a):
    width = a.shape[1]
    lane = lanes(a.shape)
    step = 1
    while step < width:
        a = a + jnp.where(lane >= step, pltpu.roll(a, step, 1), 0.0)
        step *= 2
    return a


def suffix_sum(a):
    width = a.shape[1]
    lane = lanes(a.shape)
    step = 1
    while step < width:
        a = a + jnp.where(lane < width - step, pltpu.roll(a, width - step, 1), 0.0)
        step *= 2
    return a


def decay_rows(forget):
    return running_sum(jnp.minimum(forget, 0.0) - jnp.log1p(jnp.exp(-jnp.abs(forget))))


def to_columns(tile):
    full = jnp.concatenate([tile, jnp.zeros((120, tile.shape[1]), F32)], axis=0)
    return full.T


def summary_kernel(k_ref, v_ref, ig_ref, fg_ref, out_ref):
    decay = decay_rows(fg_ref[...])
    total = decay[:, T - 1 : T]
    source = total - decay + ig_ref[...]
    peak = jnp.max(source, axis=1, keepdims=True)
    scale = jnp.exp(source - peak)
    for h in range(2):
        keys = k_ref[:, h * DK : (h + 1) * DK].astype(F32).T
        scaled = keys * scale[h : h + 1]
        normal = jnp.sum(scaled, axis=1, keepdims=True)
        memory = jnp.dot(
            scaled.astype(BF16), v_ref[:, h * DH : (h + 1) * DH], preferred_element_type=F32
        )
        held = slice(h * DK, (h + 1) * DK)
        out_ref[held, :DH] = memory.astype(BF16)
        ones = jnp.ones((DK, 1), F32)
        parts = split3(normal)
        parts += split3(ones * jnp.maximum(total[h : h + 1], LOWEST))
        parts += split3(ones * peak[h : h + 1])
        out_ref[held, DH:] = place(parts, (DK, 128)).astype(BF16)


def combine_kernel(in_ref, out_ref):
    size = BLOCKS * SLICE
    tile = in_ref[:, DH:].astype(F32)
    across = tile.T
    decay = (across[3:4] + across[4:5]) + across[5:6]
    peak = (across[6:7] + across[7:8]) + across[8:9]
    shape = (BLOCKS, size)
    block, lane = rows(shape), lanes(shape)
    source = lax.shift_right_logical(lane, 3)
    earlier = source < block
    head_lane = (lane & (SLICE - 1)) == 0
    held = jnp.where(earlier & head_lane, decay, 0.0)
    total = jnp.sum(held, axis=1, keepdims=True)
    after = suffix_sum(jnp.where(lane < size - 1, pltpu.roll(held, size - 1, 1), 0.0))
    weight = peak + after
    running = jnp.maximum(
        total, jnp.max(jnp.where(earlier, weight, LOWEST), axis=1, keepdims=True)
    )
    factor = jnp.where(earlier, jnp.exp(jnp.minimum(weight - running, 0.0)), 0.0)
    spread = (
        lax.shift_right_logical(rows((size, BLOCKS)), 3) == lanes((size, BLOCKS))
    ).astype(BF16)
    same = (rows((size, size)) & (SLICE - 1)) == (lanes((size, size)) & (SLICE - 1))
    memory = jnp.zeros((size, DH), F32)
    scalars = jnp.zeros((size, 128), F32)
    for i, part in enumerate(split3(factor)):
        wide = jnp.dot(spread, part.astype(BF16), preferred_element_type=F32)
        wide = jnp.where(same, wide, 0.0).astype(BF16)
        scalars += jnp.dot(wide, in_ref[:, DH:], preferred_element_type=F32)
        if i < 2:
            memory += jnp.dot(wide, in_ref[:, :DH], preferred_element_type=F32)
    out_ref[:, :DH] = memory.astype(BF16)
    peaks = place(split3(running), (BLOCKS, 128)).astype(BF16)
    peaks = jnp.dot(spread, peaks, preferred_element_type=F32)
    normal = pick(scalars, 0, 3)
    entries = split3(normal) + split3(pick(peaks, 0, 3))
    out_ref[:, DH:] = place(entries, (size, 128)).astype(BF16)


def intra_kernel(q_ref, k_ref, v_ref, ig_ref, fg_ref, numer_ref, terms_ref):
    decay = decay_rows(fg_ref[...])
    offset = ig_ref[...]
    columns = to_columns(jnp.concatenate([decay, jnp.zeros((6, T), F32)], axis=0))
    causal = rows((T, T)) >= lanes((T, T))
    terms = []
    for h in range(2):
        scores = (
            lax.dot_general(
                q_ref[:, h * DK : (h + 1) * DK],
                k_ref[:, h * DK : (h + 1) * DK],
                (((1,), (1,)), ((), ())),
                preferred_element_type=F32,
            )
            * SCALE
        )
        own = columns[:, h : h + 1]
        logits = own - decay[h : h + 1] + offset[h : h + 1]
        logits = jnp.where(causal, logits, -jnp.inf)
        row_peak = jnp.max(logits, axis=1, keepdims=True)
        weights = (jnp.exp(logits - row_peak) * scores).astype(BF16)
        numer_ref[:, h * DH : (h + 1) * DH] = jnp.dot(
            weights, v_ref[:, h * DH : (h + 1) * DH], preferred_element_type=F32
        )
        terms += [own, row_peak, jnp.sum(weights.astype(F32), axis=1, keepdims=True)]
    terms_ref[...] = place(terms, (T, 128))


def readout_kernel(q_ref, m_ref, numer_ref, terms_ref, out_ref):
    terms = terms_ref[...]
    for h in range(2):
        own, row_peak, denom = (terms[:, 3 * h + i : 3 * h + i + 1] for i in range(3))
        held = slice(h * DK, (h + 1) * DK)
        peak = pick(m_ref[h * DK : h * DK + 8, DH:].astype(F32), 3, 3)[:1]
        read = jnp.dot(q_ref[:, held], m_ref[held], preferred_element_type=F32) * SCALE
        prior = own + peak
        ceiling = jnp.maximum(prior, row_peak)
        prior_scale = jnp.exp(prior - ceiling)
        local_scale = jnp.exp(row_peak - ceiling)
        columns = slice(h * DH, (h + 1) * DH)
        numerator = prior_scale * read[:, :DH] + local_scale * numer_ref[:, columns]
        denominator = prior_scale * pick(read[:, DH:], 0, 3) + local_scale * denom
        floor_value = jnp.maximum(jnp.abs(denominator), 1.0)
        out_ref[:, columns] = (numerator / floor_value).astype(BF16)


def project_kernel(where_ref, own_ref, other_ref, *refs):
    pieces, (send_ref, keep_ref, held, sems) = refs[:8], refs[8:]
    x, c = where_ref[0], where_ref[1]
    copies = []
    for half in range(2):
        for r in range(4):
            dst = held.at[(c + half) & 1, (x + r) & 3]
            copy = pltpu.make_async_copy(pieces[half * 4 + r], dst, sems.at[half * 4 + r])
            copy.start()
            copies.append(copy)
    for copy in copies:
        copy.wait()

    def part(rows_ref, half, block):
        return lax.dot_general(
            rows_ref[:, half * 512 : (half + 1) * 512],
            held[half, block],
            (((1,), (1,)), ((), ())),
            preferred_element_type=F32,
        )

    def total(own_block, other_block):
        out = part(own_ref, 0, own_block) + part(own_ref, 1, own_block)
        return out + part(other_ref, 0, other_block) + part(other_ref, 1, other_block)

    send_ref[...] = total(where_ref[2], where_ref[3]).astype(BF16)
    keep_ref[...] = total(where_ref[4], where_ref[5])


def call(kernel, out_shape, *operands, **kwargs):
    return pl.pallas_call(
        kernel,
        out_shape=out_shape,
        compiler_params=pltpu.CompilerParams(vmem_limit_bytes=48 * 1024 * 1024),
        **kwargs,
    )(*operands)


def shape(rows_, columns, dtype):
    return jax.ShapeDtypeStruct((rows_, columns), dtype)


def exchange_blocks(a):
    pairs = []
    for x in range(4):
        for h in range(4):
            outer = h in (0, 3)
            if outer and x in (1, 2):
                to = ({1: 0, 2: 3}[x], h ^ 1)
            elif not outer and x in (0, 3):
                to = ({0: 1, 3: 2}[x], h ^ 1)
            else:
                to = (x, h)
            pairs.append((x * 4 + h, to[0] * 4 + to[1]))
    return lax.ppermute(a, ("x", "h"), pairs)


def shifted(a, axis, by, size=4):
    return lax.ppermute(a, axis, [((i + by) % size, i) for i in range(size)])


def weight_pieces(out_weight):
    y, z, c = (lax.axis_index(n) for n in ("y", "z", "c"))
    columns = exchange_blocks(out_weight.T)
    low, high = columns[:, :512], columns[:, 512:]
    mine = jnp.where(c == 0, low, high)
    others = jnp.where(c == 0, high, low)
    place_of = [(zz, cc) for zz in range(2) for cc in range(2)]

    def swap(a, dz, dc):
        moves = [
            (i, place_of.index(((zz + dz) % 2, (cc + dc) % 2))) for i, (zz, cc) in enumerate(place_of)
        ]
        return lax.ppermute(a, ("z", "c"), moves)

    near = swap(others, 0, 1)
    far_same = swap(mine, 1, 0)
    far_other = swap(others, 1, 1)
    here = jnp.where(c == 0, jnp.concatenate([mine, near]), jnp.concatenate([near, mine]))
    there = jnp.where(
        c == 0, jnp.concatenate([far_same, far_other]), jnp.concatenate([far_other, far_same])
    )
    group = jnp.where(z == 0, jnp.concatenate([here, there]), jnp.concatenate([there, here]))
    ring = [group] + [shifted(group, "y", by) for by in (1, 2, 3)]
    ring = jnp.stack(ring + ring[:3])
    plane = lax.dynamic_slice_in_dim(ring, (4 - y) % 4, 4, 0).reshape(1024, 512)
    first = [plane] + [shifted(plane, "x", by) for by in (1, 2, 3)]
    second = [lax.ppermute(a, "c", [(0, 1), (1, 0)]) for a in first]
    return first + second


def per_device(queries, key_rows, value_rows, input_gate, forget_gate, out_weight):
    pieces = weight_pieces(out_weight)
    gate_in, gate_forget = input_gate.T, forget_gate.T
    summary = call(
        summary_kernel, shape(T, EXT, BF16), key_rows, value_rows, gate_in, gate_forget
    )
    grouped = lax.all_to_all(summary.reshape(BLOCKS, SLICE, EXT), SEQ, 0, 0, tiled=True)
    entering = call(combine_kernel, shape(T, EXT, BF16), grouped.reshape(T, EXT))
    carried = lax.all_to_all(entering.reshape(BLOCKS, SLICE, EXT), SEQ, 0, 0, tiled=True)
    carried = carried.reshape(T, EXT)
    numer, terms = call(
        intra_kernel,
        (shape(T, 2 * DH, F32), shape(T, 128, F32)),
        queries, key_rows, value_rows, gate_in, gate_forget,
    )

    x, c, h = (lax.axis_index(n) for n in ("x", "c", "h"))
    outer = (h == 0) | (h == 3)
    keep = (h >= 2).astype(jnp.int32)

    def block(half, is_outer):
        return jnp.where(is_outer, 3 * half, 1 + half)

    where = jnp.stack(
        [x, c, block(1 - keep, outer), block(1 - keep, ~outer), block(keep, outer), block(keep, ~outer)]
    ).astype(jnp.int32)
    size = T // CHUNKS
    any_spec = pl.BlockSpec(memory_space=pl.ANY)
    vmem = pl.BlockSpec(memory_space=pltpu.VMEM)
    outs = []
    for i in range(CHUNKS):
        rows_of = lambda a: lax.slice_in_dim(a, i * size, (i + 1) * size, axis=0)
        hidden = call(
            readout_kernel, shape(size, 2 * DH, BF16),
            rows_of(queries), carried, rows_of(numer), rows_of(terms),
        )
        other = lax.ppermute(hidden, "h", [(j, j ^ 1) for j in range(4)])
        send, kept = call(
            project_kernel,
            (shape(size, 1024, BF16), shape(size, 1024, F32)),
            where, hidden, other, *pieces,
            in_specs=[pl.BlockSpec(memory_space=pltpu.SMEM), vmem, vmem] + [any_spec] * 8,
            out_specs=(vmem, vmem),
            scratch_shapes=[
                pltpu.VMEM((2, 4, 1024, 512), BF16),
                pltpu.SemaphoreType.DMA((8,)),
            ],
        )
        arrived = lax.ppermute(send, "h", [(j, 3 - j) for j in range(4)])
        outs.append((kept + arrived.astype(F32)).astype(BF16))
    return jnp.concatenate(outs, axis=0)


def solution(mesh):
    fine = Mesh(mesh.devices.reshape(4, 4, 2, 2, 4), SEQ + ("h",))
    both = P(SEQ, "h")
    return jax.shard_map(
        per_device,
        mesh=fine,
        in_specs=(both,) * 5 + (P("h", SEQ),),
        out_specs=both,
        check_vma=False,
    )
```

```python
import functools

import jax
import jax.numpy as jnp
import numpy as np
from jax import lax
from jax.experimental import pallas as pl
from jax.experimental.pallas import tpu as pltpu
from jax.sharding import Mesh, PartitionSpec as P

DH = 512
DK = 256
T = 512
BLOCKS = 64
SLICE = 8
EXT = DH + 128
SEQ = ("x", "y", "z", "c")
CHUNKS = 4
F32 = jnp.float32
BF16 = jnp.bfloat16
SCALE = DK ** (-0.5)
LOWEST = -1e30


def split3(a):
    hi = a.astype(BF16).astype(F32)
    rest = a - hi
    mid = rest.astype(BF16).astype(F32)
    return hi, mid, rest - mid


def lanes(shape):
    return lax.broadcasted_iota(jnp.int32, shape, len(shape) - 1)


def rows(shape):
    return lax.broadcasted_iota(jnp.int32, shape, 0)


def place(columns, shape):
    lane = lanes(shape)
    out = jnp.zeros(shape, F32)
    for i, column in enumerate(columns):
        out = jnp.where(lane == i, column, out)
    return out


def pick(tile, first, count):
    lane = lanes(tile.shape)
    keep = (lane >= first) & (lane < first + count)
    return jnp.sum(jnp.where(keep, tile, 0.0), axis=1, keepdims=True)


def running_sum(a):
    width = a.shape[1]
    lane = lanes(a.shape)
    step = 1
    while step < width:
        a = a + jnp.where(lane >= step, pltpu.roll(a, step, 1), 0.0)
        step *= 2
    return a


def suffix_sum(a):
    width = a.shape[1]
    lane = lanes(a.shape)
    step = 1
    while step < width:
        a = a + jnp.where(lane < width - step, pltpu.roll(a, width - step, 1), 0.0)
        step *= 2
    return a


def decay_rows(forget):
    return running_sum(jnp.minimum(forget, 0.0) - jnp.log1p(jnp.exp(-jnp.abs(forget))))


def to_columns(tile):
    full = jnp.concatenate([tile, jnp.zeros((120, tile.shape[1]), F32)], axis=0)
    return full.T


def load(pairs, sems):
    copies = [pltpu.make_async_copy(a, b, sems.at[i]) for i, (a, b) in enumerate(pairs)]
    for copy in copies:
        copy.start()
    return copies


def summary_kernel(k_hbm, v_hbm, ig_hbm, fg_hbm, *refs):
    out_ref, k_ref, v_ref, ig_ref, fg_ref, sems = refs[-6:]
    copies = load(
        ((fg_hbm, fg_ref), (ig_hbm, ig_ref), (k_hbm, k_ref), (v_hbm, v_ref)), sems
    )
    for copy in copies[:2]:
        copy.wait()
    decay = decay_rows(fg_ref[...])
    total = decay[:, T - 1 : T]
    source = total - decay + ig_ref[...]
    peak = jnp.max(source, axis=1, keepdims=True)
    scale = jnp.exp(source - peak)
    for copy in copies[2:]:
        copy.wait()
    for h in range(2):
        keys = k_ref[:, h * DK : (h + 1) * DK].astype(F32).T
        scaled = keys * scale[h : h + 1]
        normal = jnp.sum(scaled, axis=1, keepdims=True)
        memory = jnp.dot(
            scaled.astype(BF16), v_ref[:, h * DH : (h + 1) * DH], preferred_element_type=F32
        )
        held = slice(h * DK, (h + 1) * DK)
        out_ref[held, :DH] = memory.astype(BF16)
        ones = jnp.ones((DK, 1), F32)
        parts = split3(normal)
        parts += split3(ones * jnp.maximum(total[h : h + 1], LOWEST))
        parts += split3(ones * peak[h : h + 1])
        out_ref[held, DH:] = place(parts, (DK, 128)).astype(BF16)


def combine_kernel(in_ref, *refs):
    out_ref = refs[-1]
    size = BLOCKS * SLICE
    tile = in_ref[:, DH:].astype(F32)
    across = tile.T
    decay = (across[3:4] + across[4:5]) + across[5:6]
    peak = (across[6:7] + across[7:8]) + across[8:9]
    shape = (BLOCKS, size)
    block, lane = rows(shape), lanes(shape)
    source = lax.shift_right_logical(lane, 3)
    earlier = source < block
    head_lane = (lane & (SLICE - 1)) == 0
    held = jnp.where(earlier & head_lane, decay, 0.0)
    total = jnp.sum(held, axis=1, keepdims=True)
    after = suffix_sum(jnp.where(lane < size - 1, pltpu.roll(held, size - 1, 1), 0.0))
    weight = peak + after
    running = jnp.maximum(
        total, jnp.max(jnp.where(earlier, weight, LOWEST), axis=1, keepdims=True)
    )
    factor = jnp.where(earlier, jnp.exp(jnp.minimum(weight - running, 0.0)), 0.0)
    spread = (
        lax.shift_right_logical(rows((size, BLOCKS)), 3) == lanes((size, BLOCKS))
    ).astype(BF16)
    same = (rows((size, size)) & (SLICE - 1)) == (lanes((size, size)) & (SLICE - 1))
    memory = jnp.zeros((size, DH), F32)
    scalars = jnp.zeros((size, 128), F32)
    for i, part in enumerate(split3(factor)):
        wide = jnp.dot(spread, part.astype(BF16), preferred_element_type=F32)
        wide = jnp.where(same, wide, 0.0).astype(BF16)
        scalars += jnp.dot(wide, in_ref[:, DH:], preferred_element_type=F32)
        if i < 2:
            memory += jnp.dot(wide, in_ref[:, :DH], preferred_element_type=F32)
    out_ref[:, :DH] = memory.astype(BF16)
    peaks = place(split3(running), (BLOCKS, 128)).astype(BF16)
    peaks = jnp.dot(spread, peaks, preferred_element_type=F32)
    normal = pick(scalars, 0, 3)
    entries = split3(normal) + split3(pick(peaks, 0, 3))
    out_ref[:, DH:] = place(entries, (size, 128)).astype(BF16)


def intra_kernel(q_hbm, k_hbm, v_hbm, ig_hbm, fg_hbm, _, numer_hbm, terms_hbm, *scratch):
    q_ref, k_ref, v_ref, ig_ref, fg_ref, numer_ref, terms_ref, sems = scratch
    copies = load(
        (
            (fg_hbm, fg_ref), (ig_hbm, ig_ref), (q_hbm, q_ref), (k_hbm, k_ref), (v_hbm, v_ref),
        ),
        sems,
    )
    for copy in copies[:2]:
        copy.wait()
    decay = decay_rows(fg_ref[...])
    offset = ig_ref[...]
    columns = to_columns(jnp.concatenate([decay, jnp.zeros((6, T), F32)], axis=0))
    causal = rows((T, T)) >= lanes((T, T))
    for copy in copies[2:]:
        copy.wait()
    terms = []
    stores = []
    for h in range(2):
        scores = (
            lax.dot_general(
                q_ref[:, h * DK : (h + 1) * DK],
                k_ref[:, h * DK : (h + 1) * DK],
                (((1,), (1,)), ((), ())),
                preferred_element_type=F32,
            )
            * SCALE
        )
        own = columns[:, h : h + 1]
        logits = own - decay[h : h + 1] + offset[h : h + 1]
        logits = jnp.where(causal, logits, -jnp.inf)
        row_peak = jnp.max(logits, axis=1, keepdims=True)
        weights = (jnp.exp(logits - row_peak) * scores).astype(BF16)
        held = numer_ref.at[:, h * DH : (h + 1) * DH]
        held[...] = jnp.dot(weights, v_ref[:, h * DH : (h + 1) * DH], preferred_element_type=F32)
        store = pltpu.make_async_copy(
            held, numer_hbm.at[:, h * DH : (h + 1) * DH], sems.at[5 + h]
        )
        store.start()
        stores.append(store)
        terms += [own, row_peak, jnp.sum(weights.astype(F32), axis=1, keepdims=True)]
    terms_ref[...] = place(terms, (T, 128))
    store = pltpu.make_async_copy(terms_ref, terms_hbm, sems.at[7])
    store.start()
    for store in stores + [store]:
        store.wait()


def readout_kernel(start, q_hbm, m_hbm, numer_hbm, terms_hbm, out_ref, *scratch):
    q_ref, m_ref, numer_ref, terms_ref, sems = scratch
    mine = pl.ds(start, out_ref.shape[0])
    copies = load(
        (
            (m_hbm, m_ref), (q_hbm.at[mine], q_ref),
            (terms_hbm.at[mine], terms_ref), (numer_hbm.at[mine], numer_ref),
        ),
        sems,
    )
    for copy in copies:
        copy.wait()
    terms = terms_ref[...]
    for h in range(2):
        own, row_peak, denom = (terms[:, 3 * h + i : 3 * h + i + 1] for i in range(3))
        held = slice(h * DK, (h + 1) * DK)
        peak = pick(m_ref[h * DK : h * DK + 8, DH:].astype(F32), 3, 3)[:1]
        read = jnp.dot(q_ref[:, held], m_ref[held], preferred_element_type=F32) * SCALE
        prior = own + peak
        ceiling = jnp.maximum(prior, row_peak)
        prior_scale = jnp.exp(prior - ceiling)
        local_scale = jnp.exp(row_peak - ceiling)
        columns = slice(h * DH, (h + 1) * DH)
        numerator = prior_scale * read[:, :DH] + local_scale * numer_ref[:, columns]
        denominator = prior_scale * pick(read[:, DH:], 0, 3) + local_scale * denom
        floor_value = jnp.maximum(jnp.abs(denominator), 1.0)
        out_ref[:, columns] = (numerator / floor_value).astype(BF16)


def order_kernel(*refs):
    pass


def group_kernel(where_ref, *refs):
    pieces, out_ref = refs[:4], refs[-1]
    for i, piece in enumerate(pieces):
        slot = where_ref[2] ^ i
        out_ref[pl.ds(pl.multiple_of(slot * 64, 64), 64)] = piece[...]


def ring_kernel(where_ref, *refs):
    pieces, out_ref = refs[:4], refs[-1]
    start = jnp.where((where_ref[2] & 1) == 0, where_ref[1], where_ref[0])
    for r, piece in enumerate(pieces):
        out_ref[(start + r) & 3] = piece[...]


def product(first, where_ref, own_ref, other_ref, pieces, held, sems):
    x, y, c = where_ref[0], where_ref[1], where_ref[2] & 1
    blocks = (where_ref[first], where_ref[first + 1])

    def fetch(along_x, along_y):
        for s in range(2):
            for r in range(4):
                @pl.when(((x + r) & 3) == blocks[s])
                def _():
                    pltpu.make_async_copy(along_x[r], held.at[0, s], sems.at[s]).start()
        for s in range(2):
            for r in range(4):
                pltpu.make_async_copy(
                    along_y[r].at[blocks[s]], held.at[1, s, (y + r) & 3], sems.at[2 + s]
                ).start()

    @pl.when(c == 0)
    def _():
        fetch(pieces[:4], pieces[4:])

    @pl.when(c == 1)
    def _():
        fetch(pieces[4:], pieces[:4])

    total = jnp.zeros((own_ref.shape[0], 1024), F32)
    for half in range(2):
        for s, rows_ref in enumerate((own_ref, other_ref)):
            block = held.at[half, s]
            pltpu.make_async_copy(block, block, sems.at[2 * half + s]).wait()
            total += lax.dot_general(
                rows_ref[:, half * 512 : (half + 1) * 512],
                block[...].reshape(1024, 512),
                (((1,), (1,)), ((), ())),
                preferred_element_type=F32,
            )
    return total


def project_kernel(first, where_ref, own_ref, other_ref, *refs):
    out_ref, held, sems = refs[-3:]
    total = product(first, where_ref, own_ref, other_ref, refs[:8], held, sems)
    out_ref[...] = total.astype(out_ref.dtype)


def finish_kernel(start, where_ref, own_ref, other_ref, arrived_ref, *refs):
    out_hbm, held, sems, staged = refs[-4:]
    total = product(5, where_ref, own_ref, other_ref, refs[:8], held, sems)
    staged[...] = (total + arrived_ref[...].astype(F32)).astype(BF16)
    rows_out = out_hbm.at[pl.ds(start, staged.shape[0])]
    pltpu.async_copy(staged, rows_out, sems.at[0]).wait()


def add_kernel(start, kept_ref, arrived_ref, _, out_hbm, staged, sem):
    staged[...] = (kept_ref[...] + arrived_ref[...].astype(F32)).astype(BF16)
    pltpu.async_copy(staged, out_hbm.at[pl.ds(start, staged.shape[0])], sem).wait()


def call(kernel, out_shape, *operands, cost_us=None, **kwargs):
    if cost_us is not None:
        kwargs["cost_estimate"] = pl.CostEstimate(
            flops=0, bytes_accessed=int(cost_us * 3.7e6), transcendentals=0
        )
    return pl.pallas_call(
        kernel,
        out_shape=out_shape,
        compiler_params=pltpu.CompilerParams(vmem_limit_bytes=16 * 1024 * 1024),
        **kwargs,
    )(*operands)


def shape(rows_, columns, dtype):
    return jax.ShapeDtypeStruct((rows_, columns), dtype)


SIZES = (4, 4, 2, 2, 4)
NAMES = SEQ + ("h",)
ANY = pl.BlockSpec(memory_space=pl.ANY)
VMEM = pl.BlockSpec(memory_space=pltpu.VMEM)
SMEM = pl.BlockSpec(memory_space=pltpu.SMEM)
HBM = pl.BlockSpec(memory_space=pltpu.MemorySpace.HBM)
SEM = pltpu.SemaphoreType.DMA


def fetch(a, source_of):
    places = [tuple(int(i) for i in p) for p in np.ndindex(*SIZES)]
    index = {p: i for i, p in enumerate(places)}
    return lax.ppermute(a, NAMES, [(index[source_of(*p)], index[p]) for p in places])


def paired(x, h):
    outer = h in (0, 3)
    moves = {1: 0, 2: 3} if outer else {0: 1, 3: 2}
    return (moves[x], h ^ 1) if x in moves else (x, h)


def along(turned, r):
    def source_of(x, y, z, c, h):
        if (c == 1) ^ turned:
            return ((x + r) % 4, y, z, c, h)
        return (x, (y + r) % 4, z, c, h)

    return source_of


def pinned(*arrays):
    return [pltpu.with_memory_space_constraint(a, pltpu.MemorySpace.HBM) for a in arrays]


def order(a, *after):
    return call(
        order_kernel, jax.ShapeDtypeStruct(a.shape, a.dtype), a, *after,
        in_specs=[ANY] * (1 + len(after)), out_specs=ANY, input_output_aliases={0: 0},
    )


def weight_near(out_weight):
    c = lax.axis_index("c")
    columns = out_weight.T
    low, high = columns[:, :512], columns[:, 512:]
    halves = (jnp.where(c == 0, low, high), jnp.where(c == 0, high, low))

    def source_of(dz, dc):
        def of(x, y, z, c, h):
            sx, sh = paired(x, h)
            return (sx, y, z ^ dz, c ^ dc, sh)

        return of

    return [fetch(halves[dc], source_of(dz, dc)) for dz in range(2) for dc in range(2)]


def per_device(queries, key_rows, value_rows, input_gate, forget_gate, out_weight):
    x, y, z, c, h = (lax.axis_index(n) for n in NAMES)
    outer = (h == 0) | (h == 3)
    keep = (h >= 2).astype(jnp.int32)

    def block(half, is_outer):
        return jnp.where(is_outer, 3 * half, 1 + half)

    where = jnp.stack(
        [
            x, y, 2 * z + c,
            block(1 - keep, outer), block(1 - keep, ~outer),
            block(keep, outer), block(keep, ~outer),
        ]
    ).astype(jnp.int32)

    near = weight_near(out_weight)
    gates = (input_gate.T, forget_gate.T)
    gate_space = [pltpu.VMEM((2, T), F32)] * 2
    summary = call(
        summary_kernel, shape(T, EXT, BF16), *pinned(key_rows, value_rows, *gates),
        in_specs=[HBM] * 4, out_specs=VMEM,
        scratch_shapes=[
            pltpu.VMEM((T, 2 * DK), BF16), pltpu.VMEM((T, 2 * DH), BF16), *gate_space, SEM((4,)),
        ],
    )
    grouped = lax.all_to_all(summary.reshape(BLOCKS, SLICE, EXT), SEQ, 0, 0, tiled=True)
    group = call(
        group_kernel, shape(256, 512, BF16), where, *near, summary,
        in_specs=[SMEM] + [VMEM] * 4 + [ANY], out_specs=VMEM,
    )
    ring = [group] + [fetch(group, along(False, r)) for r in (1, 2, 3)]
    entering = call(
        combine_kernel, shape(T, EXT, BF16), grouped.reshape(T, EXT), group,
        in_specs=[VMEM, ANY], out_specs=VMEM, cost_us=0.1,
    )
    carried = lax.all_to_all(entering.reshape(BLOCKS, SLICE, EXT), SEQ, 0, 0, tiled=True)
    carried = carried.reshape(T, EXT)
    plane = call(
        ring_kernel, jax.ShapeDtypeStruct((4, 256, 512), BF16), where, *ring, entering,
        in_specs=[SMEM] + [VMEM] * 4 + [ANY], out_specs=VMEM, cost_us=20,
    )
    pieces = [plane] + [fetch(plane, along(True, r)) for r in (1, 2, 3)]
    numer, terms = call(
        intra_kernel,
        (pltpu.MemorySpace.HBM((T, 2 * DH), F32), pltpu.MemorySpace.HBM((T, 128), F32)),
        *pinned(queries, key_rows, value_rows, *gates), plane,
        in_specs=[HBM] * 5 + [ANY], out_specs=(HBM, HBM), cost_us=0.1,
        scratch_shapes=[
            pltpu.VMEM((T, 2 * DK), BF16), pltpu.VMEM((T, 2 * DK), BF16),
            pltpu.VMEM((T, 2 * DH), BF16), *gate_space,
            pltpu.VMEM((T, 2 * DH), F32), pltpu.VMEM((T, 128), F32), SEM((8,)),
        ],
    )

    size = T // CHUNKS
    hiddens = []
    for i in range(CHUNKS):
        hiddens.append(call(
            functools.partial(readout_kernel, i * size), shape(size, 2 * DH, BF16),
            *pinned(queries, carried, numer, terms),
            in_specs=[HBM] * 4, out_specs=VMEM,
            scratch_shapes=[
                pltpu.VMEM((size, 2 * DK), BF16), pltpu.VMEM((T, EXT), BF16),
                pltpu.VMEM((size, 2 * DH), F32), pltpu.VMEM((size, 128), F32), SEM((4,)),
            ],
        ))
    first = lax.ppermute(hiddens[0], "h", [(j, j ^ 1) for j in range(4)])
    pieces = pieces[:1] + [order(a, first) for a in pieces[1:]]
    pieces += [lax.ppermute(a, "c", [(0, 1), (1, 0)]) for a in pieces]
    held = [pltpu.VMEM((2, 2, 4, 256, 512), BF16), SEM((4,))]
    staged = pltpu.VMEM((size, 1024), BF16)

    def project(first, dtype, hidden, other, *after):
        return call(
            functools.partial(project_kernel, first), shape(size, 1024, dtype),
            where, hidden, other, *pieces, *after,
            in_specs=[SMEM, VMEM, VMEM] + [ANY] * (8 + len(after)), out_specs=VMEM,
            scratch_shapes=held,
        )

    out = None
    others, sends, arrivals = [], [], []
    for i, hidden in enumerate(hiddens):
        if i > 0:
            hidden = order(hidden, others[i - 1], *sends[max(i - 2, 0) : i - 1])
            other = lax.ppermute(hidden, "h", [(j, j ^ 1) for j in range(4)])
        else:
            other = first
        send = project(3, BF16, hidden, other)
        if i > 0:
            send = order(send, arrivals[i - 1])
        arrived = lax.ppermute(send, "h", [(j, 3 - j) for j in range(4)])
        others.append(other)
        sends.append(send)
        arrivals.append(arrived)
        before = [] if out is None else [out]
        if i < CHUNKS - 1:
            out = call(
                functools.partial(finish_kernel, i * size), shape(T, 1024, BF16),
                where, hidden, other, arrived, *pieces, *before,
                in_specs=[SMEM, VMEM, VMEM, VMEM] + [ANY] * 8 + [HBM] * len(before),
                out_specs=HBM, scratch_shapes=held + [staged],
                input_output_aliases={12: 0} if before else {},
            )
        else:
            out = call(
                functools.partial(add_kernel, i * size), shape(T, 1024, BF16),
                project(5, F32, hidden, other), arrived, out,
                in_specs=[VMEM, VMEM, HBM], out_specs=HBM,
                scratch_shapes=[staged, SEM], input_output_aliases={2: 0},
            )
    return out


def solution(mesh):
    fine = Mesh(mesh.devices.reshape(4, 4, 2, 2, 4), SEQ + ("h",))
    both = P(SEQ, "h")
    return jax.shard_map(
        per_device,
        mesh=fine,
        in_specs=(both,) * 5 + (P("h", SEQ),),
        out_specs=both,
        check_vma=False,
    )
```

```python
import functools

import jax
import jax.numpy as jnp
import numpy as np
from jax import lax
from jax.experimental import pallas as pl
from jax.experimental.pallas import tpu as pltpu
from jax.sharding import Mesh, PartitionSpec as P

DH = 512
DK = 256
T = 512
BLOCKS = 64
SLICE = 8
EXT = DH + 128
SEQ = ("x", "y", "z", "c")
SIZES_OUT = (128, 192, 192)
F32 = jnp.float32
BF16 = jnp.bfloat16
SCALE = DK ** (-0.5)
LOWEST = -1e30


def split3(a):
    hi = a.astype(BF16).astype(F32)
    rest = a - hi
    mid = rest.astype(BF16).astype(F32)
    return hi, mid, rest - mid


def lanes(shape):
    return lax.broadcasted_iota(jnp.int32, shape, len(shape) - 1)


def rows(shape):
    return lax.broadcasted_iota(jnp.int32, shape, 0)


def place(columns, shape):
    lane = lanes(shape)
    out = jnp.zeros(shape, F32)
    for i, column in enumerate(columns):
        out = jnp.where(lane == i, column, out)
    return out


def pick(tile, first, count):
    lane = lanes(tile.shape)
    keep = (lane >= first) & (lane < first + count)
    return jnp.sum(jnp.where(keep, tile, 0.0), axis=1, keepdims=True)


def running_sum(a):
    width = a.shape[1]
    lane = lanes(a.shape)
    step = 1
    while step < width:
        a = a + jnp.where(lane >= step, pltpu.roll(a, step, 1), 0.0)
        step *= 2
    return a


def suffix_sum(a):
    width = a.shape[1]
    lane = lanes(a.shape)
    step = 1
    while step < width:
        a = a + jnp.where(lane < width - step, pltpu.roll(a, width - step, 1), 0.0)
        step *= 2
    return a


def decay_rows(forget):
    return running_sum(jnp.minimum(forget, 0.0) - jnp.log1p(jnp.exp(-jnp.abs(forget))))


def to_columns(tile):
    full = jnp.concatenate([tile, jnp.zeros((120, tile.shape[1]), F32)], axis=0)
    return full.T


def load(pairs, sems):
    copies = [pltpu.make_async_copy(a, b, sems.at[i]) for i, (a, b) in enumerate(pairs)]
    for copy in copies:
        copy.start()
    return copies


def summary_kernel(k_hbm, v_hbm, ig_hbm, fg_hbm, *refs):
    out_ref, k_ref, v_ref, ig_ref, fg_ref, sems = refs[-6:]
    copies = load(
        ((fg_hbm, fg_ref), (ig_hbm, ig_ref), (k_hbm, k_ref), (v_hbm, v_ref)), sems
    )
    for copy in copies[:2]:
        copy.wait()
    decay = decay_rows(fg_ref[...])
    total = decay[:, T - 1 : T]
    source = total - decay + ig_ref[...]
    peak = jnp.max(source, axis=1, keepdims=True)
    scale = jnp.exp(source - peak)
    for copy in copies[2:]:
        copy.wait()
    for h in range(2):
        keys = k_ref[:, h * DK : (h + 1) * DK].astype(F32).T
        scaled = keys * scale[h : h + 1]
        normal = jnp.sum(scaled, axis=1, keepdims=True)
        memory = jnp.dot(
            scaled.astype(BF16), v_ref[:, h * DH : (h + 1) * DH], preferred_element_type=F32
        )
        held = slice(h * DK, (h + 1) * DK)
        out_ref[held, :DH] = memory.astype(BF16)
        ones = jnp.ones((DK, 1), F32)
        parts = split3(normal)
        parts += split3(ones * jnp.maximum(total[h : h + 1], LOWEST))
        parts += split3(ones * peak[h : h + 1])
        out_ref[held, DH:] = place(parts, (DK, 128)).astype(BF16)


def combine_kernel(in_ref, *refs):
    out_ref = refs[-1]
    size = BLOCKS * SLICE
    tile = in_ref[:, DH:].astype(F32)
    across = tile.T
    decay = (across[3:4] + across[4:5]) + across[5:6]
    peak = (across[6:7] + across[7:8]) + across[8:9]
    shape = (BLOCKS, size)
    block, lane = rows(shape), lanes(shape)
    source = lax.shift_right_logical(lane, 3)
    earlier = source < block
    head_lane = (lane & (SLICE - 1)) == 0
    held = jnp.where(earlier & head_lane, decay, 0.0)
    total = jnp.sum(held, axis=1, keepdims=True)
    after = suffix_sum(jnp.where(lane < size - 1, pltpu.roll(held, size - 1, 1), 0.0))
    weight = peak + after
    running = jnp.maximum(
        total, jnp.max(jnp.where(earlier, weight, LOWEST), axis=1, keepdims=True)
    )
    factor = jnp.where(earlier, jnp.exp(jnp.minimum(weight - running, 0.0)), 0.0)
    spread = (
        lax.shift_right_logical(rows((size, BLOCKS)), 3) == lanes((size, BLOCKS))
    ).astype(BF16)
    same = (rows((size, size)) & (SLICE - 1)) == (lanes((size, size)) & (SLICE - 1))
    memory = jnp.zeros((size, DH), F32)
    scalars = jnp.zeros((size, 128), F32)
    for i, part in enumerate(split3(factor)):
        wide = jnp.dot(spread, part.astype(BF16), preferred_element_type=F32)
        wide = jnp.where(same, wide, 0.0).astype(BF16)
        scalars += jnp.dot(wide, in_ref[:, DH:], preferred_element_type=F32)
        if i < 2:
            memory += jnp.dot(wide, in_ref[:, :DH], preferred_element_type=F32)
    out_ref[:, :DH] = memory.astype(BF16)
    peaks = place(split3(running), (BLOCKS, 128)).astype(BF16)
    peaks = jnp.dot(spread, peaks, preferred_element_type=F32)
    normal = pick(scalars, 0, 3)
    entries = split3(normal) + split3(pick(peaks, 0, 3))
    out_ref[:, DH:] = place(entries, (size, 128)).astype(BF16)


def intra_kernel(q_hbm, k_hbm, v_hbm, ig_hbm, fg_hbm, _, numer_hbm, terms_hbm, *scratch):
    q_ref, k_ref, v_ref, ig_ref, fg_ref, numer_ref, terms_ref, sems = scratch
    copies = load(
        (
            (fg_hbm, fg_ref), (ig_hbm, ig_ref), (q_hbm, q_ref), (k_hbm, k_ref), (v_hbm, v_ref),
        ),
        sems,
    )
    for copy in copies[:2]:
        copy.wait()
    decay = decay_rows(fg_ref[...])
    offset = ig_ref[...]
    columns = to_columns(jnp.concatenate([decay, jnp.zeros((6, T), F32)], axis=0))
    causal = rows((T, T)) >= lanes((T, T))
    for copy in copies[2:]:
        copy.wait()
    terms = []
    stores = []
    for h in range(2):
        scores = (
            lax.dot_general(
                q_ref[:, h * DK : (h + 1) * DK],
                k_ref[:, h * DK : (h + 1) * DK],
                (((1,), (1,)), ((), ())),
                preferred_element_type=F32,
            )
            * SCALE
        )
        own = columns[:, h : h + 1]
        logits = own - decay[h : h + 1] + offset[h : h + 1]
        logits = jnp.where(causal, logits, -jnp.inf)
        row_peak = jnp.max(logits, axis=1, keepdims=True)
        weights = (jnp.exp(logits - row_peak) * scores).astype(BF16)
        held = numer_ref.at[:, h * DH : (h + 1) * DH]
        held[...] = jnp.dot(weights, v_ref[:, h * DH : (h + 1) * DH], preferred_element_type=F32)
        store = pltpu.make_async_copy(
            held, numer_hbm.at[:, h * DH : (h + 1) * DH], sems.at[5 + h]
        )
        store.start()
        stores.append(store)
        terms += [own, row_peak, jnp.sum(weights.astype(F32), axis=1, keepdims=True)]
    terms_ref[...] = place(terms, (T, 128))
    store = pltpu.make_async_copy(terms_ref, terms_hbm, sems.at[7])
    store.start()
    for store in stores + [store]:
        store.wait()


def readout_kernel(start, q_hbm, m_hbm, numer_hbm, terms_hbm, *refs):
    out_ref, q_ref, m_ref, numer_ref, terms_ref, sems = refs[-6:]
    mine = pl.ds(start, out_ref.shape[0])
    copies = load(
        (
            (m_hbm, m_ref), (q_hbm.at[mine], q_ref),
            (terms_hbm.at[mine], terms_ref), (numer_hbm.at[mine], numer_ref),
        ),
        sems,
    )
    for copy in copies:
        copy.wait()
    terms = terms_ref[...]
    for h in range(2):
        own, row_peak, denom = (terms[:, 3 * h + i : 3 * h + i + 1] for i in range(3))
        held = slice(h * DK, (h + 1) * DK)
        peak = pick(m_ref[h * DK : h * DK + 8, DH:].astype(F32), 3, 3)[:1]
        read = jnp.dot(q_ref[:, held], m_ref[held], preferred_element_type=F32) * SCALE
        prior = own + peak
        ceiling = jnp.maximum(prior, row_peak)
        prior_scale = jnp.exp(prior - ceiling)
        local_scale = jnp.exp(row_peak - ceiling)
        columns = slice(h * DH, (h + 1) * DH)
        numerator = prior_scale * read[:, :DH] + local_scale * numer_ref[:, columns]
        denominator = prior_scale * pick(read[:, DH:], 0, 3) + local_scale * denom
        floor_value = jnp.maximum(jnp.abs(denominator), 1.0)
        out_ref[:, columns] = (numerator / floor_value).astype(BF16)


def order_kernel(*refs):
    pass


def group_kernel(where_ref, *refs):
    pieces, out_ref = refs[:4], refs[-1]
    for i, piece in enumerate(pieces):
        slot = where_ref[2] ^ i
        out_ref[pl.ds(pl.multiple_of(slot * 64, 64), 64)] = piece[...]


def ring_kernel(where_ref, *refs):
    pieces, out_ref = refs[:4], refs[-1]
    start = jnp.where((where_ref[2] & 1) == 0, where_ref[1], where_ref[0])
    for r, piece in enumerate(pieces):
        out_ref[(start + r) & 3] = piece[...]


def product(first, where_ref, own_ref, other_ref, pieces, held, sems):
    x, y, c = where_ref[0], where_ref[1], where_ref[2] & 1
    blocks = (where_ref[first], where_ref[first + 1])

    def fetch(along_x, along_y):
        for s in range(2):
            for r in range(4):
                @pl.when(((x + r) & 3) == blocks[s])
                def _():
                    pltpu.make_async_copy(along_x[r], held.at[0, s], sems.at[s]).start()
        for s in range(2):
            for r in range(4):
                pltpu.make_async_copy(
                    along_y[r].at[blocks[s]], held.at[1, s, (y + r) & 3], sems.at[2 + s]
                ).start()

    @pl.when(c == 0)
    def _():
        fetch(pieces[:4], pieces[4:])

    @pl.when(c == 1)
    def _():
        fetch(pieces[4:], pieces[:4])

    total = jnp.zeros((own_ref.shape[0], 1024), F32)
    for half in range(2):
        for s, rows_ref in enumerate((own_ref, other_ref)):
            block = held.at[half, s]
            pltpu.make_async_copy(block, block, sems.at[2 * half + s]).wait()
            total += lax.dot_general(
                rows_ref[:, half * 512 : (half + 1) * 512],
                block[...].reshape(1024, 512),
                (((1,), (1,)), ((), ())),
                preferred_element_type=F32,
            )
    return total


def project_kernel(first, where_ref, own_ref, other_ref, *refs):
    out_ref, held, sems = refs[-3:]
    total = product(first, where_ref, own_ref, other_ref, refs[:8], held, sems)
    out_ref[...] = total.astype(out_ref.dtype)


def finish_kernel(start, where_ref, own_ref, other_ref, arrived_ref, *refs):
    out_hbm, held, sems, staged = refs[-4:]
    total = product(5, where_ref, own_ref, other_ref, refs[:8], held, sems)
    staged[...] = (total + arrived_ref[...].astype(F32)).astype(BF16)
    rows_out = out_hbm.at[pl.ds(start, staged.shape[0])]
    pltpu.async_copy(staged, rows_out, sems.at[0]).wait()


def add_kernel(start, kept_ref, arrived_ref, _, out_hbm, staged, sem):
    staged[...] = (kept_ref[...] + arrived_ref[...].astype(F32)).astype(BF16)
    pltpu.async_copy(staged, out_hbm.at[pl.ds(start, staged.shape[0])], sem).wait()


def call(kernel, out_shape, *operands, **kwargs):
    return pl.pallas_call(
        kernel,
        out_shape=out_shape,
        compiler_params=pltpu.CompilerParams(vmem_limit_bytes=16 * 1024 * 1024),
        **kwargs,
    )(*operands)


def shape(rows_, columns, dtype):
    return jax.ShapeDtypeStruct((rows_, columns), dtype)


SIZES = (4, 4, 2, 2, 4)
NAMES = SEQ + ("h",)
ANY = pl.BlockSpec(memory_space=pl.ANY)
VMEM = pl.BlockSpec(memory_space=pltpu.VMEM)
SMEM = pl.BlockSpec(memory_space=pltpu.SMEM)
HBM = pl.BlockSpec(memory_space=pltpu.MemorySpace.HBM)
SEM = pltpu.SemaphoreType.DMA


def fetch(a, source_of):
    places = [tuple(int(i) for i in p) for p in np.ndindex(*SIZES)]
    index = {p: i for i, p in enumerate(places)}
    return lax.ppermute(a, NAMES, [(index[source_of(*p)], index[p]) for p in places])


def paired(x, h):
    outer = h in (0, 3)
    moves = {1: 0, 2: 3} if outer else {0: 1, 3: 2}
    return (moves[x], h ^ 1) if x in moves else (x, h)


def along(turned, r):
    def source_of(x, y, z, c, h):
        if (c == 1) ^ turned:
            return ((x + r) % 4, y, z, c, h)
        return (x, (y + r) % 4, z, c, h)

    return source_of


def pinned(*arrays):
    return [pltpu.with_memory_space_constraint(a, pltpu.MemorySpace.HBM) for a in arrays]


def order(a, *after):
    return call(
        order_kernel, jax.ShapeDtypeStruct(a.shape, a.dtype), a, *after,
        in_specs=[ANY] * (1 + len(after)), out_specs=ANY, input_output_aliases={0: 0},
    )


def weight_near(out_weight):
    c = lax.axis_index("c")
    columns = out_weight.T
    low, high = columns[:, :512], columns[:, 512:]
    halves = (jnp.where(c == 0, low, high), jnp.where(c == 0, high, low))

    def source_of(dz, dc):
        def of(x, y, z, c, h):
            sx, sh = paired(x, h)
            return (sx, y, z ^ dz, c ^ dc, sh)

        return of

    return [fetch(halves[dc], source_of(dz, dc)) for dz in range(2) for dc in range(2)]


def per_device(queries, key_rows, value_rows, input_gate, forget_gate, out_weight):
    x, y, z, c, h = (lax.axis_index(n) for n in NAMES)
    outer = (h == 0) | (h == 3)
    keep = (h >= 2).astype(jnp.int32)

    def block(half, is_outer):
        return jnp.where(is_outer, 3 * half, 1 + half)

    where = jnp.stack(
        [
            x, y, 2 * z + c,
            block(1 - keep, outer), block(1 - keep, ~outer),
            block(keep, outer), block(keep, ~outer),
        ]
    ).astype(jnp.int32)

    near = weight_near(out_weight)
    gates = (input_gate.T, forget_gate.T)
    gate_space = [pltpu.VMEM((2, T), F32)] * 2
    summary = call(
        summary_kernel, shape(T, EXT, BF16), *pinned(key_rows, value_rows, *gates),
        in_specs=[HBM] * 4, out_specs=VMEM,
        scratch_shapes=[
            pltpu.VMEM((T, 2 * DK), BF16), pltpu.VMEM((T, 2 * DH), BF16), *gate_space, SEM((4,)),
        ],
    )
    grouped = lax.all_to_all(summary.reshape(BLOCKS, SLICE, EXT), SEQ, 0, 0, tiled=True)
    group = call(
        group_kernel, shape(256, 512, BF16), where, *near, summary,
        in_specs=[SMEM] + [VMEM] * 4 + [ANY], out_specs=VMEM,
    )
    ring = [group] + [fetch(group, along(False, r)) for r in (1, 2, 3)]
    plane = call(
        ring_kernel, jax.ShapeDtypeStruct((4, 256, 512), BF16), where, *ring,
        in_specs=[SMEM] + [VMEM] * 4, out_specs=VMEM,
    )
    pieces = [plane] + [fetch(plane, along(True, r)) for r in (1, 2, 3)]
    numer, terms = call(
        intra_kernel,
        (pltpu.MemorySpace.HBM((T, 2 * DH), F32), pltpu.MemorySpace.HBM((T, 128), F32)),
        *pinned(queries, key_rows, value_rows, *gates), near[3],
        in_specs=[HBM] * 5 + [ANY], out_specs=(HBM, HBM),
        scratch_shapes=[
            pltpu.VMEM((T, 2 * DK), BF16), pltpu.VMEM((T, 2 * DK), BF16),
            pltpu.VMEM((T, 2 * DH), BF16), *gate_space,
            pltpu.VMEM((T, 2 * DH), F32), pltpu.VMEM((T, 128), F32), SEM((8,)),
        ],
    )
    entering = call(
        combine_kernel, shape(T, EXT, BF16), grouped.reshape(T, EXT), plane, terms,
        in_specs=[VMEM, ANY, ANY], out_specs=VMEM,
    )
    carried = lax.all_to_all(entering.reshape(BLOCKS, SLICE, EXT), SEQ, 0, 0, tiled=True)
    carried = carried.reshape(T, EXT)

    starts = [sum(SIZES_OUT[:i]) for i in range(len(SIZES_OUT))]
    hiddens = []
    for start, size in zip(starts, SIZES_OUT):
        hiddens.append(call(
            functools.partial(readout_kernel, start), shape(size, 2 * DH, BF16),
            *pinned(queries, carried, numer, terms), *hiddens[-1:],
            in_specs=[HBM] * 4 + [ANY] * min(len(hiddens), 1), out_specs=VMEM,
            scratch_shapes=[
                pltpu.VMEM((size, 2 * DK), BF16), pltpu.VMEM((T, EXT), BF16),
                pltpu.VMEM((size, 2 * DH), F32), pltpu.VMEM((size, 128), F32), SEM((4,)),
            ],
        ))
    first = lax.ppermute(hiddens[0], "h", [(j, j ^ 1) for j in range(4)])
    pieces = pieces[:1] + [order(a, first, hiddens[-1]) for a in pieces[1:]]
    pieces += [lax.ppermute(a, "c", [(0, 1), (1, 0)]) for a in pieces]
    held = [pltpu.VMEM((2, 2, 4, 256, 512), BF16), SEM((4,))]

    def project(first, dtype, hidden, other, *after):
        return call(
            functools.partial(project_kernel, first), shape(hidden.shape[0], 1024, dtype),
            where, hidden, other, *pieces, *after,
            in_specs=[SMEM, VMEM, VMEM] + [ANY] * (8 + len(after)), out_specs=VMEM,
            scratch_shapes=held,
        )

    out = None
    others, sends, arrivals = [], [], []
    for i, start in enumerate(starts):
        hidden = hiddens[i]
        other = first if i == 0 else lax.ppermute(hidden, "h", [(j, j ^ 1) for j in range(4)])
        others.append(other)
        after = []
        if i + 1 < len(hiddens):
            after = [other, *sends[max(i - 1, 0) : i]]
            hiddens[i + 1] = order(hiddens[i + 1], *after)
            after = hiddens[i + 1 : i + 2] if i == 0 else []
        send = project(3, BF16, hidden, other, *after)
        if i > 0:
            send = order(send, arrivals[i - 1])
        arrived = lax.ppermute(send, "h", [(j, 3 - j) for j in range(4)])
        sends.append(send)
        arrivals.append(arrived)
        before = [] if out is None else [out]
        staged = pltpu.VMEM((hidden.shape[0], 1024), BF16)
        if i < len(SIZES_OUT) - 1:
            out = call(
                functools.partial(finish_kernel, start), shape(T, 1024, BF16),
                where, hidden, other, arrived, *pieces, *before,
                in_specs=[SMEM, VMEM, VMEM, VMEM] + [ANY] * 8 + [HBM] * len(before),
                out_specs=HBM, scratch_shapes=held + [staged],
                input_output_aliases={12: 0} if before else {},
            )
        else:
            out = call(
                functools.partial(add_kernel, start), shape(T, 1024, BF16),
                project(5, F32, hidden, other), arrived, out,
                in_specs=[VMEM, VMEM, HBM], out_specs=HBM,
                scratch_shapes=[staged, SEM], input_output_aliases={2: 0},
            )
    return out


def solution(mesh):
    fine = Mesh(mesh.devices.reshape(4, 4, 2, 2, 4), SEQ + ("h",))
    both = P(SEQ, "h")
    return jax.shard_map(
        per_device,
        mesh=fine,
        in_specs=(both,) * 5 + (P("h", SEQ),),
        out_specs=both,
        check_vma=False,
    )
```

```python
import functools

import jax
import jax.numpy as jnp
import numpy as np
from jax import lax
from jax.experimental import pallas as pl
from jax.experimental.pallas import tpu as pltpu
from jax.sharding import Mesh, PartitionSpec as P

DH = 512
DK = 256
T = 512
BLOCKS = 64
SLICE = 8
EXT = DH + 128
SEQ = ("x", "y", "z", "c")
SIZES_OUT = (176, 176, 160)
F32 = jnp.float32
BF16 = jnp.bfloat16
SCALE = DK ** (-0.5)
LOWEST = -1e30


def split3(a):
    hi = a.astype(BF16).astype(F32)
    rest = a - hi
    mid = rest.astype(BF16).astype(F32)
    return hi, mid, rest - mid


def lanes(shape):
    return lax.broadcasted_iota(jnp.int32, shape, len(shape) - 1)


def rows(shape):
    return lax.broadcasted_iota(jnp.int32, shape, 0)


def place(columns, shape):
    lane = lanes(shape)
    out = jnp.zeros(shape, F32)
    for i, column in enumerate(columns):
        out = jnp.where(lane == i, column, out)
    return out


def pick(tile, first, count):
    lane = lanes(tile.shape)
    keep = (lane >= first) & (lane < first + count)
    return jnp.sum(jnp.where(keep, tile, 0.0), axis=1, keepdims=True)


def running_sum(a):
    width = a.shape[1]
    lane = lanes(a.shape)
    step = 1
    while step < width:
        a = a + jnp.where(lane >= step, pltpu.roll(a, step, 1), 0.0)
        step *= 2
    return a


def suffix_sum(a):
    width = a.shape[1]
    lane = lanes(a.shape)
    step = 1
    while step < width:
        a = a + jnp.where(lane < width - step, pltpu.roll(a, width - step, 1), 0.0)
        step *= 2
    return a


def decay_rows(forget):
    return running_sum(jnp.minimum(forget, 0.0) - jnp.log1p(jnp.exp(-jnp.abs(forget))))


def to_columns(tile):
    full = jnp.concatenate([tile, jnp.zeros((120, tile.shape[1]), F32)], axis=0)
    return full.T


def load(pairs, sems):
    copies = [pltpu.make_async_copy(a, b, sems.at[i]) for i, (a, b) in enumerate(pairs)]
    for copy in copies:
        copy.start()
    return copies


def summary_kernel(k_hbm, v_hbm, ig_hbm, fg_hbm, *refs):
    out_ref, k_ref, v_ref, ig_ref, fg_ref, sems = refs[-6:]
    copies = load(
        ((fg_hbm, fg_ref), (ig_hbm, ig_ref), (k_hbm, k_ref), (v_hbm, v_ref)), sems
    )
    for copy in copies[:2]:
        copy.wait()
    decay = decay_rows(fg_ref[...])
    total = decay[:, T - 1 : T]
    source = total - decay + ig_ref[...]
    peak = jnp.max(source, axis=1, keepdims=True)
    scale = jnp.exp(source - peak)
    for copy in copies[2:]:
        copy.wait()
    for h in range(2):
        keys = k_ref[:, h * DK : (h + 1) * DK].astype(F32).T
        scaled = keys * scale[h : h + 1]
        normal = jnp.sum(scaled, axis=1, keepdims=True)
        memory = jnp.dot(
            scaled.astype(BF16), v_ref[:, h * DH : (h + 1) * DH], preferred_element_type=F32
        )
        held = slice(h * DK, (h + 1) * DK)
        out_ref[held, :DH] = memory.astype(BF16)
        ones = jnp.ones((DK, 1), F32)
        parts = split3(normal)
        parts += split3(ones * jnp.maximum(total[h : h + 1], LOWEST))
        parts += split3(ones * peak[h : h + 1])
        out_ref[held, DH:] = place(parts, (DK, 128)).astype(BF16)


def combine_kernel(in_ref, *refs):
    out_ref = refs[-1]
    size = BLOCKS * SLICE
    tile = in_ref[:, DH:].astype(F32)
    across = tile.T
    decay = (across[3:4] + across[4:5]) + across[5:6]
    peak = (across[6:7] + across[7:8]) + across[8:9]
    shape = (BLOCKS, size)
    block, lane = rows(shape), lanes(shape)
    source = lax.shift_right_logical(lane, 3)
    earlier = source < block
    head_lane = (lane & (SLICE - 1)) == 0
    held = jnp.where(earlier & head_lane, decay, 0.0)
    total = jnp.sum(held, axis=1, keepdims=True)
    after = suffix_sum(jnp.where(lane < size - 1, pltpu.roll(held, size - 1, 1), 0.0))
    weight = peak + after
    running = jnp.maximum(
        total, jnp.max(jnp.where(earlier, weight, LOWEST), axis=1, keepdims=True)
    )
    factor = jnp.where(earlier, jnp.exp(jnp.minimum(weight - running, 0.0)), 0.0)
    spread = (
        lax.shift_right_logical(rows((size, BLOCKS)), 3) == lanes((size, BLOCKS))
    ).astype(BF16)
    same = (rows((size, size)) & (SLICE - 1)) == (lanes((size, size)) & (SLICE - 1))
    memory = jnp.zeros((size, DH), F32)
    scalars = jnp.zeros((size, 128), F32)
    for i, part in enumerate(split3(factor)):
        wide = jnp.dot(spread, part.astype(BF16), preferred_element_type=F32)
        wide = jnp.where(same, wide, 0.0).astype(BF16)
        scalars += jnp.dot(wide, in_ref[:, DH:], preferred_element_type=F32)
        if i < 2:
            memory += jnp.dot(wide, in_ref[:, :DH], preferred_element_type=F32)
    out_ref[:, :DH] = memory.astype(BF16)
    peaks = place(split3(running), (BLOCKS, 128)).astype(BF16)
    peaks = jnp.dot(spread, peaks, preferred_element_type=F32)
    normal = pick(scalars, 0, 3)
    entries = split3(normal) + split3(pick(peaks, 0, 3))
    out_ref[:, DH:] = place(entries, (size, 128)).astype(BF16)


def intra_kernel(q_hbm, k_hbm, v_hbm, ig_hbm, fg_hbm, _, numer_hbm, terms_hbm, *scratch):
    q_ref, k_ref, v_ref, ig_ref, fg_ref, numer_ref, terms_ref, sems = scratch
    copies = load(
        (
            (fg_hbm, fg_ref), (ig_hbm, ig_ref), (q_hbm, q_ref), (k_hbm, k_ref), (v_hbm, v_ref),
        ),
        sems,
    )
    for copy in copies[:2]:
        copy.wait()
    decay = decay_rows(fg_ref[...])
    offset = ig_ref[...]
    columns = to_columns(jnp.concatenate([decay, jnp.zeros((6, T), F32)], axis=0))
    causal = rows((T, T)) >= lanes((T, T))
    for copy in copies[2:]:
        copy.wait()
    terms = []
    stores = []
    for h in range(2):
        scores = (
            lax.dot_general(
                q_ref[:, h * DK : (h + 1) * DK],
                k_ref[:, h * DK : (h + 1) * DK],
                (((1,), (1,)), ((), ())),
                preferred_element_type=F32,
            )
            * SCALE
        )
        own = columns[:, h : h + 1]
        logits = own - decay[h : h + 1] + offset[h : h + 1]
        logits = jnp.where(causal, logits, -jnp.inf)
        row_peak = jnp.max(logits, axis=1, keepdims=True)
        weights = (jnp.exp(logits - row_peak) * scores).astype(BF16)
        held = numer_ref.at[:, h * DH : (h + 1) * DH]
        held[...] = jnp.dot(weights, v_ref[:, h * DH : (h + 1) * DH], preferred_element_type=F32)
        store = pltpu.make_async_copy(
            held, numer_hbm.at[:, h * DH : (h + 1) * DH], sems.at[5 + h]
        )
        store.start()
        stores.append(store)
        terms += [own, row_peak, jnp.sum(weights.astype(F32), axis=1, keepdims=True)]
    terms_ref[...] = place(terms, (T, 128))
    store = pltpu.make_async_copy(terms_ref, terms_hbm, sems.at[7])
    store.start()
    for store in stores + [store]:
        store.wait()


def readout_kernel(start, q_hbm, m_hbm, numer_hbm, terms_hbm, *refs):
    out_ref, q_ref, m_ref, numer_ref, terms_ref, sems = refs[-6:]
    mine = pl.ds(start, out_ref.shape[0])
    copies = load(
        (
            (m_hbm, m_ref), (q_hbm.at[mine], q_ref),
            (terms_hbm.at[mine], terms_ref), (numer_hbm.at[mine], numer_ref),
        ),
        sems,
    )
    for copy in copies:
        copy.wait()
    terms = terms_ref[...]
    for h in range(2):
        own, row_peak, denom = (terms[:, 3 * h + i : 3 * h + i + 1] for i in range(3))
        held = slice(h * DK, (h + 1) * DK)
        peak = pick(m_ref[h * DK : h * DK + 8, DH:].astype(F32), 3, 3)[:1]
        read = jnp.dot(q_ref[:, held], m_ref[held], preferred_element_type=F32) * SCALE
        prior = own + peak
        ceiling = jnp.maximum(prior, row_peak)
        prior_scale = jnp.exp(prior - ceiling)
        local_scale = jnp.exp(row_peak - ceiling)
        columns = slice(h * DH, (h + 1) * DH)
        numerator = prior_scale * read[:, :DH] + local_scale * numer_ref[:, columns]
        denominator = prior_scale * pick(read[:, DH:], 0, 3) + local_scale * denom
        floor_value = jnp.maximum(jnp.abs(denominator), 1.0)
        out_ref[:, columns] = (numerator / floor_value).astype(BF16)


def order_kernel(*refs):
    pass


def group_kernel(where_ref, *refs):
    pieces, out_ref = refs[:4], refs[-1]
    for i, piece in enumerate(pieces):
        slot = where_ref[2] ^ i
        out_ref[pl.ds(pl.multiple_of(slot * 64, 64), 64)] = piece[...]


def ring_kernel(where_ref, *refs):
    pieces, out_ref = refs[:4], refs[-1]
    start = jnp.where((where_ref[2] & 1) == 0, where_ref[1], where_ref[0])
    for r, piece in enumerate(pieces):
        out_ref[(start + r) & 3] = piece[...]


def product(first, where_ref, own_ref, other_ref, pieces, held, sems):
    x, y, c = where_ref[0], where_ref[1], where_ref[2] & 1
    blocks = (where_ref[first], where_ref[first + 1])

    def fetch(along_x, along_y):
        for s in range(2):
            for r in range(4):
                @pl.when(((x + r) & 3) == blocks[s])
                def _():
                    pltpu.make_async_copy(along_x[r], held.at[0, s], sems.at[s]).start()
        for s in range(2):
            for r in range(4):
                pltpu.make_async_copy(
                    along_y[r].at[blocks[s]], held.at[1, s, (y + r) & 3], sems.at[2 + s]
                ).start()

    @pl.when(c == 0)
    def _():
        fetch(pieces[:4], pieces[4:])

    @pl.when(c == 1)
    def _():
        fetch(pieces[4:], pieces[:4])

    total = jnp.zeros((own_ref.shape[0], 1024), F32)
    for half in range(2):
        for s, rows_ref in enumerate((own_ref, other_ref)):
            block = held.at[half, s]
            pltpu.make_async_copy(block, block, sems.at[2 * half + s]).wait()
            total += lax.dot_general(
                rows_ref[:, half * 512 : (half + 1) * 512],
                block[...].reshape(1024, 512),
                (((1,), (1,)), ((), ())),
                preferred_element_type=F32,
            )
    return total


def project_kernel(first, where_ref, own_ref, other_ref, *refs):
    out_ref, held, sems = refs[-3:]
    total = product(first, where_ref, own_ref, other_ref, refs[:8], held, sems)
    out_ref[...] = total.astype(out_ref.dtype)


def finish_kernel(start, where_ref, own_ref, other_ref, arrived_ref, *refs):
    out_hbm, held, sems, staged = refs[-4:]
    total = product(5, where_ref, own_ref, other_ref, refs[:8], held, sems)
    staged[...] = (total + arrived_ref[...].astype(F32)).astype(BF16)
    rows_out = out_hbm.at[pl.ds(start, staged.shape[0])]
    pltpu.async_copy(staged, rows_out, sems.at[0]).wait()


def add_kernel(start, kept_ref, arrived_ref, _, out_hbm, staged, sem):
    staged[...] = (kept_ref[...] + arrived_ref[...].astype(F32)).astype(BF16)
    pltpu.async_copy(staged, out_hbm.at[pl.ds(start, staged.shape[0])], sem).wait()


def call(kernel, out_shape, *operands, **kwargs):
    return pl.pallas_call(
        kernel,
        out_shape=out_shape,
        compiler_params=pltpu.CompilerParams(vmem_limit_bytes=16 * 1024 * 1024),
        **kwargs,
    )(*operands)


def shape(rows_, columns, dtype):
    return jax.ShapeDtypeStruct((rows_, columns), dtype)


SIZES = (4, 4, 2, 2, 4)
NAMES = SEQ + ("h",)
ANY = pl.BlockSpec(memory_space=pl.ANY)
VMEM = pl.BlockSpec(memory_space=pltpu.VMEM)
SMEM = pl.BlockSpec(memory_space=pltpu.SMEM)
HBM = pl.BlockSpec(memory_space=pltpu.MemorySpace.HBM)
SEM = pltpu.SemaphoreType.DMA


def fetch(a, source_of):
    places = [tuple(int(i) for i in p) for p in np.ndindex(*SIZES)]
    index = {p: i for i, p in enumerate(places)}
    return lax.ppermute(a, NAMES, [(index[source_of(*p)], index[p]) for p in places])


def paired(x, h):
    outer = h in (0, 3)
    moves = {1: 0, 2: 3} if outer else {0: 1, 3: 2}
    return (moves[x], h ^ 1) if x in moves else (x, h)


def along(turned, r):
    def source_of(x, y, z, c, h):
        if (c == 1) ^ turned:
            return ((x + r) % 4, y, z, c, h)
        return (x, (y + r) % 4, z, c, h)

    return source_of


def pinned(*arrays):
    return [pltpu.with_memory_space_constraint(a, pltpu.MemorySpace.HBM) for a in arrays]


def order(a, *after):
    return call(
        order_kernel, jax.ShapeDtypeStruct(a.shape, a.dtype), a, *after,
        in_specs=[ANY] * (1 + len(after)), out_specs=ANY, input_output_aliases={0: 0},
    )


def weight_near(out_weight):
    c = lax.axis_index("c")
    columns = out_weight.T
    low, high = columns[:, :512], columns[:, 512:]
    halves = (jnp.where(c == 0, low, high), jnp.where(c == 0, high, low))

    def source_of(dz, dc):
        def of(x, y, z, c, h):
            sx, sh = paired(x, h)
            return (sx, y, z ^ dz, c ^ dc, sh)

        return of

    return [fetch(halves[dc], source_of(dz, dc)) for dz in range(2) for dc in range(2)]


def per_device(queries, key_rows, value_rows, input_gate, forget_gate, out_weight):
    x, y, z, c, h = (lax.axis_index(n) for n in NAMES)
    outer = (h == 0) | (h == 3)
    keep = (h >= 2).astype(jnp.int32)

    def block(half, is_outer):
        return jnp.where(is_outer, 3 * half, 1 + half)

    where = jnp.stack(
        [
            x, y, 2 * z + c,
            block(1 - keep, outer), block(1 - keep, ~outer),
            block(keep, outer), block(keep, ~outer),
        ]
    ).astype(jnp.int32)

    near = weight_near(out_weight)
    gates = (input_gate.T, forget_gate.T)
    gate_space = [pltpu.VMEM((2, T), F32)] * 2
    summary = call(
        summary_kernel, shape(T, EXT, BF16), *pinned(key_rows, value_rows, *gates),
        in_specs=[HBM] * 4, out_specs=VMEM,
        scratch_shapes=[
            pltpu.VMEM((T, 2 * DK), BF16), pltpu.VMEM((T, 2 * DH), BF16), *gate_space, SEM((4,)),
        ],
    )
    summary = order(summary, *near)
    grouped = lax.all_to_all(summary.reshape(BLOCKS, SLICE, EXT), SEQ, 0, 0, tiled=True)
    group = call(
        group_kernel, shape(256, 512, BF16), where, *near, summary,
        in_specs=[SMEM] + [VMEM] * 4 + [ANY], out_specs=VMEM,
    )
    ring = [group] + [fetch(group, along(False, r)) for r in (1, 2, 3)]
    plane = call(
        ring_kernel, jax.ShapeDtypeStruct((4, 256, 512), BF16), where, *ring,
        in_specs=[SMEM] + [VMEM] * 4, out_specs=VMEM,
    )
    pieces = [plane] + [fetch(plane, along(True, r)) for r in (1, 2, 3)]
    numer, terms = call(
        intra_kernel,
        (pltpu.MemorySpace.HBM((T, 2 * DH), F32), pltpu.MemorySpace.HBM((T, 128), F32)),
        *pinned(queries, key_rows, value_rows, *gates), group,
        in_specs=[HBM] * 5 + [ANY], out_specs=(HBM, HBM),
        scratch_shapes=[
            pltpu.VMEM((T, 2 * DK), BF16), pltpu.VMEM((T, 2 * DK), BF16),
            pltpu.VMEM((T, 2 * DH), BF16), *gate_space,
            pltpu.VMEM((T, 2 * DH), F32), pltpu.VMEM((T, 128), F32), SEM((8,)),
        ],
    )
    entering = call(
        combine_kernel, shape(T, EXT, BF16), grouped.reshape(T, EXT), plane, terms,
        in_specs=[VMEM, ANY, ANY], out_specs=VMEM,
    )
    carried = lax.all_to_all(entering.reshape(BLOCKS, SLICE, EXT), SEQ, 0, 0, tiled=True)
    carried = carried.reshape(T, EXT)

    starts = [sum(SIZES_OUT[:i]) for i in range(len(SIZES_OUT))]
    hiddens = []
    for start, size in zip(starts, SIZES_OUT):
        hiddens.append(call(
            functools.partial(readout_kernel, start), shape(size, 2 * DH, BF16),
            *pinned(queries, carried, numer, terms), *hiddens[-1:],
            in_specs=[HBM] * 4 + [ANY] * min(len(hiddens), 1), out_specs=VMEM,
            scratch_shapes=[
                pltpu.VMEM((size, 2 * DK), BF16), pltpu.VMEM((T, EXT), BF16),
                pltpu.VMEM((size, 2 * DH), F32), pltpu.VMEM((size, 128), F32), SEM((4,)),
            ],
        ))
    first = lax.ppermute(hiddens[0], "h", [(j, j ^ 1) for j in range(4)])
    pieces = pieces[:1] + [order(a, first, hiddens[-1]) for a in pieces[1:]]
    pieces += [lax.ppermute(a, "c", [(0, 1), (1, 0)]) for a in pieces]
    held = [pltpu.VMEM((2, 2, 4, 256, 512), BF16), SEM((4,))]

    def project(first, dtype, hidden, other, *after):
        return call(
            functools.partial(project_kernel, first), shape(hidden.shape[0], 1024, dtype),
            where, hidden, other, *pieces, *after,
            in_specs=[SMEM, VMEM, VMEM] + [ANY] * (8 + len(after)), out_specs=VMEM,
            scratch_shapes=held,
        )

    out = None
    others, sends, arrivals = [], [], []
    for i, start in enumerate(starts):
        hidden = hiddens[i]
        other = first if i == 0 else lax.ppermute(hidden, "h", [(j, j ^ 1) for j in range(4)])
        others.append(other)
        after = []
        if i + 1 < len(hiddens):
            after = [other, *sends[max(i - 1, 0) : i]]
            hiddens[i + 1] = order(hiddens[i + 1], *after)
            after = hiddens[i + 1 : i + 2] if i == 0 else []
        send = project(3, BF16, hidden, other, *after)
        if i > 0:
            send = order(send, arrivals[i - 1])
        arrived = lax.ppermute(send, "h", [(j, 3 - j) for j in range(4)])
        sends.append(send)
        arrivals.append(arrived)
        before = [] if out is None else [out]
        staged = pltpu.VMEM((hidden.shape[0], 1024), BF16)
        if i < len(SIZES_OUT) - 1:
            out = call(
                functools.partial(finish_kernel, start), shape(T, 1024, BF16),
                where, hidden, other, arrived, *pieces, *before,
                in_specs=[SMEM, VMEM, VMEM, VMEM] + [ANY] * 8 + [HBM] * len(before),
                out_specs=HBM, scratch_shapes=held + [staged],
                input_output_aliases={12: 0} if before else {},
            )
        else:
            out = call(
                functools.partial(add_kernel, start), shape(T, 1024, BF16),
                project(5, F32, hidden, other), arrived, out,
                in_specs=[VMEM, VMEM, HBM], out_specs=HBM,
                scratch_shapes=[staged, SEM], input_output_aliases={2: 0},
            )
    return out


def solution(mesh):
    fine = Mesh(mesh.devices.reshape(4, 4, 2, 2, 4), SEQ + ("h",))
    both = P(SEQ, "h")
    return jax.shard_map(
        per_device,
        mesh=fine,
        in_specs=(both,) * 5 + (P("h", SEQ),),
        out_specs=both,
        check_vma=False,
    )
```

```python
import functools

import jax
import jax.numpy as jnp
import numpy as np
from jax import lax
from jax.experimental import pallas as pl
from jax.experimental.pallas import tpu as pltpu
from jax.sharding import Mesh, PartitionSpec as P

DH = 512
DK = 256
T = 512
BLOCKS = 64
SLICE = 8
EXT = DH + 128
SEQ = ("x", "y", "z", "c")
SIZES_OUT = (144, 192, 176)
F32 = jnp.float32
BF16 = jnp.bfloat16
SCALE = DK ** (-0.5)
LOWEST = -1e30


def split3(a):
    hi = a.astype(BF16).astype(F32)
    rest = a - hi
    mid = rest.astype(BF16).astype(F32)
    return hi, mid, rest - mid


def lanes(shape):
    return lax.broadcasted_iota(jnp.int32, shape, len(shape) - 1)


def rows(shape):
    return lax.broadcasted_iota(jnp.int32, shape, 0)


def place(columns, shape):
    lane = lanes(shape)
    out = jnp.zeros(shape, F32)
    for i, column in enumerate(columns):
        out = jnp.where(lane == i, column, out)
    return out


def pick(tile, first, count):
    lane = lanes(tile.shape)
    keep = (lane >= first) & (lane < first + count)
    return jnp.sum(jnp.where(keep, tile, 0.0), axis=1, keepdims=True)


def running_sum(a):
    width = a.shape[1]
    lane = lanes(a.shape)
    step = 1
    while step < width:
        a = a + jnp.where(lane >= step, pltpu.roll(a, step, 1), 0.0)
        step *= 2
    return a


def suffix_sum(a):
    width = a.shape[1]
    lane = lanes(a.shape)
    step = 1
    while step < width:
        a = a + jnp.where(lane < width - step, pltpu.roll(a, width - step, 1), 0.0)
        step *= 2
    return a


def decay_rows(forget):
    return running_sum(jnp.minimum(forget, 0.0) - jnp.log1p(jnp.exp(-jnp.abs(forget))))


def to_columns(tile):
    full = jnp.concatenate([tile, jnp.zeros((120, tile.shape[1]), F32)], axis=0)
    return full.T


def load(pairs, sems):
    copies = [pltpu.make_async_copy(a, b, sems.at[i]) for i, (a, b) in enumerate(pairs)]
    for copy in copies:
        copy.start()
    return copies


def summary_kernel(k_hbm, v_hbm, ig_hbm, fg_hbm, *refs):
    out_ref, k_ref, v_ref, ig_ref, fg_ref, sems = refs[-6:]
    copies = load(
        ((fg_hbm, fg_ref), (ig_hbm, ig_ref), (k_hbm, k_ref), (v_hbm, v_ref)), sems
    )
    for copy in copies[:2]:
        copy.wait()
    decay = decay_rows(fg_ref[...])
    total = decay[:, T - 1 : T]
    source = total - decay + ig_ref[...]
    peak = jnp.max(source, axis=1, keepdims=True)
    scale = jnp.exp(source - peak)
    for copy in copies[2:]:
        copy.wait()
    for h in range(2):
        keys = k_ref[:, h * DK : (h + 1) * DK].astype(F32).T
        scaled = keys * scale[h : h + 1]
        normal = jnp.sum(scaled, axis=1, keepdims=True)
        memory = jnp.dot(
            scaled.astype(BF16), v_ref[:, h * DH : (h + 1) * DH], preferred_element_type=F32
        )
        held = slice(h * DK, (h + 1) * DK)
        out_ref[held, :DH] = memory.astype(BF16)
        ones = jnp.ones((DK, 1), F32)
        parts = split3(normal)
        parts += split3(ones * jnp.maximum(total[h : h + 1], LOWEST))
        parts += split3(ones * peak[h : h + 1])
        out_ref[held, DH:] = place(parts, (DK, 128)).astype(BF16)


def combine_kernel(in_ref, *refs):
    out_ref = refs[-1]
    size = BLOCKS * SLICE
    tile = in_ref[:, DH:].astype(F32)
    across = tile.T
    decay = (across[3:4] + across[4:5]) + across[5:6]
    peak = (across[6:7] + across[7:8]) + across[8:9]
    shape = (BLOCKS, size)
    block, lane = rows(shape), lanes(shape)
    source = lax.shift_right_logical(lane, 3)
    earlier = source < block
    head_lane = (lane & (SLICE - 1)) == 0
    held = jnp.where(earlier & head_lane, decay, 0.0)
    total = jnp.sum(held, axis=1, keepdims=True)
    after = suffix_sum(jnp.where(lane < size - 1, pltpu.roll(held, size - 1, 1), 0.0))
    weight = peak + after
    running = jnp.maximum(
        total, jnp.max(jnp.where(earlier, weight, LOWEST), axis=1, keepdims=True)
    )
    factor = jnp.where(earlier, jnp.exp(jnp.minimum(weight - running, 0.0)), 0.0)
    spread = (
        lax.shift_right_logical(rows((size, BLOCKS)), 3) == lanes((size, BLOCKS))
    ).astype(BF16)
    same = (rows((size, size)) & (SLICE - 1)) == (lanes((size, size)) & (SLICE - 1))
    memory = jnp.zeros((size, DH), F32)
    scalars = jnp.zeros((size, 128), F32)
    for i, part in enumerate(split3(factor)):
        wide = jnp.dot(spread, part.astype(BF16), preferred_element_type=F32)
        wide = jnp.where(same, wide, 0.0).astype(BF16)
        scalars += jnp.dot(wide, in_ref[:, DH:], preferred_element_type=F32)
        if i < 2:
            memory += jnp.dot(wide, in_ref[:, :DH], preferred_element_type=F32)
    out_ref[:, :DH] = memory.astype(BF16)
    peaks = place(split3(running), (BLOCKS, 128)).astype(BF16)
    peaks = jnp.dot(spread, peaks, preferred_element_type=F32)
    normal = pick(scalars, 0, 3)
    entries = split3(normal) + split3(pick(peaks, 0, 3))
    out_ref[:, DH:] = place(entries, (size, 128)).astype(BF16)


def intra_kernel(q_hbm, k_hbm, v_hbm, ig_hbm, fg_hbm, _, numer_hbm, terms_hbm, *scratch):
    q_ref, k_ref, v_ref, ig_ref, fg_ref, numer_ref, terms_ref, sems = scratch
    copies = load(
        (
            (fg_hbm, fg_ref), (ig_hbm, ig_ref), (q_hbm, q_ref), (k_hbm, k_ref), (v_hbm, v_ref),
        ),
        sems,
    )
    for copy in copies[:2]:
        copy.wait()
    decay = decay_rows(fg_ref[...])
    offset = ig_ref[...]
    columns = to_columns(jnp.concatenate([decay, jnp.zeros((6, T), F32)], axis=0))
    causal = rows((T, T)) >= lanes((T, T))
    for copy in copies[2:]:
        copy.wait()
    terms = []
    stores = []
    for h in range(2):
        scores = (
            lax.dot_general(
                q_ref[:, h * DK : (h + 1) * DK],
                k_ref[:, h * DK : (h + 1) * DK],
                (((1,), (1,)), ((), ())),
                preferred_element_type=F32,
            )
            * SCALE
        )
        own = columns[:, h : h + 1]
        logits = own - decay[h : h + 1] + offset[h : h + 1]
        logits = jnp.where(causal, logits, -jnp.inf)
        row_peak = jnp.max(logits, axis=1, keepdims=True)
        weights = (jnp.exp(logits - row_peak) * scores).astype(BF16)
        held = numer_ref.at[:, h * DH : (h + 1) * DH]
        held[...] = jnp.dot(weights, v_ref[:, h * DH : (h + 1) * DH], preferred_element_type=F32)
        store = pltpu.make_async_copy(
            held, numer_hbm.at[:, h * DH : (h + 1) * DH], sems.at[5 + h]
        )
        store.start()
        stores.append(store)
        terms += [own, row_peak, jnp.sum(weights.astype(F32), axis=1, keepdims=True)]
    terms_ref[...] = place(terms, (T, 128))
    store = pltpu.make_async_copy(terms_ref, terms_hbm, sems.at[7])
    store.start()
    for store in stores + [store]:
        store.wait()


def readout_kernel(start, q_hbm, m_hbm, numer_hbm, terms_hbm, *refs):
    out_ref, q_ref, m_ref, numer_ref, terms_ref, sems = refs[-6:]
    mine = pl.ds(start, out_ref.shape[0])
    copies = load(
        (
            (m_hbm, m_ref), (q_hbm.at[mine], q_ref),
            (terms_hbm.at[mine], terms_ref), (numer_hbm.at[mine], numer_ref),
        ),
        sems,
    )
    for copy in copies:
        copy.wait()
    terms = terms_ref[...]
    for h in range(2):
        own, row_peak, denom = (terms[:, 3 * h + i : 3 * h + i + 1] for i in range(3))
        held = slice(h * DK, (h + 1) * DK)
        peak = pick(m_ref[h * DK : h * DK + 8, DH:].astype(F32), 3, 3)[:1]
        read = jnp.dot(q_ref[:, held], m_ref[held], preferred_element_type=F32) * SCALE
        prior = own + peak
        ceiling = jnp.maximum(prior, row_peak)
        prior_scale = jnp.exp(prior - ceiling)
        local_scale = jnp.exp(row_peak - ceiling)
        columns = slice(h * DH, (h + 1) * DH)
        numerator = prior_scale * read[:, :DH] + local_scale * numer_ref[:, columns]
        denominator = prior_scale * pick(read[:, DH:], 0, 3) + local_scale * denom
        floor_value = jnp.maximum(jnp.abs(denominator), 1.0)
        out_ref[:, columns] = (numerator / floor_value).astype(BF16)


def order_kernel(*refs):
    pass


def group_kernel(where_ref, *refs):
    pieces, out_ref = refs[:4], refs[-1]
    for i, piece in enumerate(pieces):
        slot = where_ref[2] ^ i
        out_ref[pl.ds(pl.multiple_of(slot * 64, 64), 64)] = piece[...]


def ring_kernel(where_ref, *refs):
    pieces, out_ref = refs[:4], refs[-1]
    start = jnp.where((where_ref[2] & 1) == 0, where_ref[1], where_ref[0])
    for r, piece in enumerate(pieces):
        out_ref[(start + r) & 3] = piece[...]


def product(first, where_ref, own_ref, other_ref, pieces, held, sems):
    x, y, c = where_ref[0], where_ref[1], where_ref[2] & 1
    blocks = (where_ref[first], where_ref[first + 1])

    def fetch(along_x, along_y):
        for s in range(2):
            for r in range(4):
                @pl.when(((x + r) & 3) == blocks[s])
                def _():
                    pltpu.make_async_copy(along_x[r], held.at[0, s], sems.at[s]).start()
        for s in range(2):
            for r in range(4):
                pltpu.make_async_copy(
                    along_y[r].at[blocks[s]], held.at[1, s, (y + r) & 3], sems.at[2 + s]
                ).start()

    @pl.when(c == 0)
    def _():
        fetch(pieces[:4], pieces[4:])

    @pl.when(c == 1)
    def _():
        fetch(pieces[4:], pieces[:4])

    total = jnp.zeros((own_ref.shape[0], 1024), F32)
    for half in range(2):
        for s, rows_ref in enumerate((own_ref, other_ref)):
            block = held.at[half, s]
            pltpu.make_async_copy(block, block, sems.at[2 * half + s]).wait()
            total += lax.dot_general(
                rows_ref[:, half * 512 : (half + 1) * 512],
                block[...].reshape(1024, 512),
                (((1,), (1,)), ((), ())),
                preferred_element_type=F32,
            )
    return total


def project_kernel(first, where_ref, own_ref, other_ref, *refs):
    out_ref, held, sems = refs[-3:]
    total = product(first, where_ref, own_ref, other_ref, refs[:8], held, sems)
    out_ref[...] = total.astype(out_ref.dtype)


def finish_kernel(start, where_ref, own_ref, other_ref, arrived_ref, *refs):
    out_hbm, held, sems, staged = refs[-4:]
    total = product(5, where_ref, own_ref, other_ref, refs[:8], held, sems)
    staged[...] = (total + arrived_ref[...].astype(F32)).astype(BF16)
    rows_out = out_hbm.at[pl.ds(start, staged.shape[0])]
    pltpu.async_copy(staged, rows_out, sems.at[0]).wait()


def add_kernel(start, kept_ref, arrived_ref, _, out_hbm, staged, sem):
    staged[...] = (kept_ref[...] + arrived_ref[...].astype(F32)).astype(BF16)
    pltpu.async_copy(staged, out_hbm.at[pl.ds(start, staged.shape[0])], sem).wait()


def call(kernel, out_shape, *operands, **kwargs):
    return pl.pallas_call(
        kernel,
        out_shape=out_shape,
        compiler_params=pltpu.CompilerParams(vmem_limit_bytes=16 * 1024 * 1024),
        **kwargs,
    )(*operands)


def shape(rows_, columns, dtype):
    return jax.ShapeDtypeStruct((rows_, columns), dtype)


SIZES = (4, 4, 2, 2, 4)
NAMES = SEQ + ("h",)
ANY = pl.BlockSpec(memory_space=pl.ANY)
VMEM = pl.BlockSpec(memory_space=pltpu.VMEM)
SMEM = pl.BlockSpec(memory_space=pltpu.SMEM)
HBM = pl.BlockSpec(memory_space=pltpu.MemorySpace.HBM)
SEM = pltpu.SemaphoreType.DMA


def fetch(a, source_of):
    places = [tuple(int(i) for i in p) for p in np.ndindex(*SIZES)]
    index = {p: i for i, p in enumerate(places)}
    return lax.ppermute(a, NAMES, [(index[source_of(*p)], index[p]) for p in places])


def paired(x, h):
    outer = h in (0, 3)
    moves = {1: 0, 2: 3} if outer else {0: 1, 3: 2}
    return (moves[x], h ^ 1) if x in moves else (x, h)


def along(turned, r):
    def source_of(x, y, z, c, h):
        if (c == 1) ^ turned:
            return ((x + r) % 4, y, z, c, h)
        return (x, (y + r) % 4, z, c, h)

    return source_of


def pinned(*arrays):
    return [pltpu.with_memory_space_constraint(a, pltpu.MemorySpace.HBM) for a in arrays]


def order(a, *after):
    return call(
        order_kernel, jax.ShapeDtypeStruct(a.shape, a.dtype), a, *after,
        in_specs=[ANY] * (1 + len(after)), out_specs=ANY, input_output_aliases={0: 0},
    )


def weight_near(out_weight):
    c = lax.axis_index("c")
    columns = out_weight.T
    low, high = columns[:, :512], columns[:, 512:]
    halves = (jnp.where(c == 0, low, high), jnp.where(c == 0, high, low))

    def source_of(dz, dc):
        def of(x, y, z, c, h):
            sx, sh = paired(x, h)
            return (sx, y, z ^ dz, c ^ dc, sh)

        return of

    return [fetch(halves[dc], source_of(dz, dc)) for dz in range(2) for dc in range(2)]


def per_device(queries, key_rows, value_rows, input_gate, forget_gate, out_weight):
    x, y, z, c, h = (lax.axis_index(n) for n in NAMES)
    outer = (h == 0) | (h == 3)
    keep = (h >= 2).astype(jnp.int32)

    def block(half, is_outer):
        return jnp.where(is_outer, 3 * half, 1 + half)

    where = jnp.stack(
        [
            x, y, 2 * z + c,
            block(1 - keep, outer), block(1 - keep, ~outer),
            block(keep, outer), block(keep, ~outer),
        ]
    ).astype(jnp.int32)

    near = weight_near(out_weight)
    gates = (input_gate.T, forget_gate.T)
    gate_space = [pltpu.VMEM((2, T), F32)] * 2
    summary = call(
        summary_kernel, shape(T, EXT, BF16), *pinned(key_rows, value_rows, *gates),
        in_specs=[HBM] * 4, out_specs=VMEM,
        scratch_shapes=[
            pltpu.VMEM((T, 2 * DK), BF16), pltpu.VMEM((T, 2 * DH), BF16), *gate_space, SEM((4,)),
        ],
    )
    grouped = lax.all_to_all(summary.reshape(BLOCKS, SLICE, EXT), SEQ, 0, 0, tiled=True)
    group = call(
        group_kernel, shape(256, 512, BF16), where, *near, summary,
        in_specs=[SMEM] + [VMEM] * 4 + [ANY], out_specs=VMEM,
    )
    ring = [group] + [fetch(group, along(False, r)) for r in (1, 2, 3)]
    plane = call(
        ring_kernel, jax.ShapeDtypeStruct((4, 256, 512), BF16), where, *ring,
        in_specs=[SMEM] + [VMEM] * 4, out_specs=VMEM,
    )
    pieces = [plane] + [fetch(plane, along(True, r)) for r in (1, 2, 3)]
    numer, terms = call(
        intra_kernel,
        (pltpu.MemorySpace.HBM((T, 2 * DH), F32), pltpu.MemorySpace.HBM((T, 128), F32)),
        *pinned(queries, key_rows, value_rows, *gates), near[3],
        in_specs=[HBM] * 5 + [ANY], out_specs=(HBM, HBM),
        scratch_shapes=[
            pltpu.VMEM((T, 2 * DK), BF16), pltpu.VMEM((T, 2 * DK), BF16),
            pltpu.VMEM((T, 2 * DH), BF16), *gate_space,
            pltpu.VMEM((T, 2 * DH), F32), pltpu.VMEM((T, 128), F32), SEM((8,)),
        ],
    )
    entering = call(
        combine_kernel, shape(T, EXT, BF16), grouped.reshape(T, EXT), plane, terms,
        in_specs=[VMEM, ANY, ANY], out_specs=VMEM,
    )
    carried = lax.all_to_all(entering.reshape(BLOCKS, SLICE, EXT), SEQ, 0, 0, tiled=True)
    carried = carried.reshape(T, EXT)

    starts = [sum(SIZES_OUT[:i]) for i in range(len(SIZES_OUT))]
    hiddens = []
    for start, size in zip(starts, SIZES_OUT):
        hiddens.append(call(
            functools.partial(readout_kernel, start), shape(size, 2 * DH, BF16),
            *pinned(queries, carried, numer, terms), *hiddens[-1:],
            in_specs=[HBM] * 4 + [ANY] * min(len(hiddens), 1), out_specs=VMEM,
            scratch_shapes=[
                pltpu.VMEM((size, 2 * DK), BF16), pltpu.VMEM((T, EXT), BF16),
                pltpu.VMEM((size, 2 * DH), F32), pltpu.VMEM((size, 128), F32), SEM((4,)),
            ],
        ))
    first = lax.ppermute(hiddens[0], "h", [(j, j ^ 1) for j in range(4)])
    pieces = [
        pieces[0], order(pieces[1], hiddens[-1]), order(pieces[2], first, hiddens[-1]),
        order(pieces[3], hiddens[-1]),
    ]
    pieces += [lax.ppermute(a, "c", [(0, 1), (1, 0)]) for a in pieces]
    held = [pltpu.VMEM((2, 2, 4, 256, 512), BF16), SEM((4,))]

    def project(first, dtype, hidden, other, *after):
        return call(
            functools.partial(project_kernel, first), shape(hidden.shape[0], 1024, dtype),
            where, hidden, other, *pieces, *after,
            in_specs=[SMEM, VMEM, VMEM] + [ANY] * (8 + len(after)), out_specs=VMEM,
            scratch_shapes=held,
        )

    out = None
    others, sends, arrivals = [], [], []
    for i, start in enumerate(starts):
        hidden = hiddens[i]
        other = first if i == 0 else lax.ppermute(hidden, "h", [(j, j ^ 1) for j in range(4)])
        others.append(other)
        after = []
        if i + 1 < len(hiddens):
            after = [other, *sends[max(i - 1, 0) : i]]
            hiddens[i + 1] = order(hiddens[i + 1], *after)
            after = hiddens[i + 1 : i + 2] if i == 0 else []
        send = project(3, BF16, hidden, other, *after)
        if i > 0:
            send = order(send, arrivals[i - 1])
        arrived = lax.ppermute(send, "h", [(j, 3 - j) for j in range(4)])
        sends.append(send)
        arrivals.append(arrived)
        before = [] if out is None else [out]
        staged = pltpu.VMEM((hidden.shape[0], 1024), BF16)
        if i < len(SIZES_OUT) - 1:
            out = call(
                functools.partial(finish_kernel, start), shape(T, 1024, BF16),
                where, hidden, other, arrived, *pieces, *before,
                in_specs=[SMEM, VMEM, VMEM, VMEM] + [ANY] * 8 + [HBM] * len(before),
                out_specs=HBM, scratch_shapes=held + [staged],
                input_output_aliases={12: 0} if before else {},
            )
        else:
            out = call(
                functools.partial(add_kernel, start), shape(T, 1024, BF16),
                project(5, F32, hidden, other), arrived, out,
                in_specs=[VMEM, VMEM, HBM], out_specs=HBM,
                scratch_shapes=[staged, SEM], input_output_aliases={2: 0},
            )
    return out


def solution(mesh):
    fine = Mesh(mesh.devices.reshape(4, 4, 2, 2, 4), SEQ + ("h",))
    both = P(SEQ, "h")
    return jax.shard_map(
        per_device,
        mesh=fine,
        in_specs=(both,) * 5 + (P("h", SEQ),),
        out_specs=both,
        check_vma=False,
    )
```

```python
import functools

import jax
import jax.numpy as jnp
import numpy as np
from jax import lax
from jax.experimental import pallas as pl
from jax.experimental.pallas import tpu as pltpu
from jax.sharding import Mesh, PartitionSpec as P

DH = 512
DK = 256
T = 512
BLOCKS = 64
SLICE = 8
EXT = DH + 128
SEQ = ("x", "y", "z", "c")
SIZES_OUT = (160, 176, 176)
F32 = jnp.float32
BF16 = jnp.bfloat16
SCALE = DK ** (-0.5)
LOWEST = -1e30


def split3(a):
    hi = a.astype(BF16).astype(F32)
    rest = a - hi
    mid = rest.astype(BF16).astype(F32)
    return hi, mid, rest - mid


def lanes(shape):
    return lax.broadcasted_iota(jnp.int32, shape, len(shape) - 1)


def rows(shape):
    return lax.broadcasted_iota(jnp.int32, shape, 0)


def place(columns, shape):
    lane = lanes(shape)
    out = jnp.zeros(shape, F32)
    for i, column in enumerate(columns):
        out = jnp.where(lane == i, column, out)
    return out


def pick(tile, first, count):
    lane = lanes(tile.shape)
    keep = (lane >= first) & (lane < first + count)
    return jnp.sum(jnp.where(keep, tile, 0.0), axis=1, keepdims=True)


def running_sum(a):
    width = a.shape[1]
    lane = lanes(a.shape)
    step = 1
    while step < width:
        a = a + jnp.where(lane >= step, pltpu.roll(a, step, 1), 0.0)
        step *= 2
    return a


def suffix_sum(a):
    width = a.shape[1]
    lane = lanes(a.shape)
    step = 1
    while step < width:
        a = a + jnp.where(lane < width - step, pltpu.roll(a, width - step, 1), 0.0)
        step *= 2
    return a


def decay_rows(forget):
    return running_sum(jnp.minimum(forget, 0.0) - jnp.log1p(jnp.exp(-jnp.abs(forget))))


def to_columns(tile):
    full = jnp.concatenate([tile, jnp.zeros((120, tile.shape[1]), F32)], axis=0)
    return full.T


def load(pairs, sems):
    copies = [pltpu.make_async_copy(a, b, sems.at[i]) for i, (a, b) in enumerate(pairs)]
    for copy in copies:
        copy.start()
    return copies


def summary_kernel(k_hbm, v_hbm, ig_hbm, fg_hbm, *refs):
    out_ref, k_ref, v_ref, ig_ref, fg_ref, sems = refs[-6:]
    copies = load(
        ((fg_hbm, fg_ref), (ig_hbm, ig_ref), (k_hbm, k_ref), (v_hbm, v_ref)), sems
    )
    for copy in copies[:2]:
        copy.wait()
    decay = decay_rows(fg_ref[...])
    total = decay[:, T - 1 : T]
    source = total - decay + ig_ref[...]
    peak = jnp.max(source, axis=1, keepdims=True)
    scale = jnp.exp(source - peak)
    for copy in copies[2:]:
        copy.wait()
    for h in range(2):
        keys = k_ref[:, h * DK : (h + 1) * DK].astype(F32).T
        scaled = keys * scale[h : h + 1]
        normal = jnp.sum(scaled, axis=1, keepdims=True)
        memory = jnp.dot(
            scaled.astype(BF16), v_ref[:, h * DH : (h + 1) * DH], preferred_element_type=F32
        )
        held = slice(h * DK, (h + 1) * DK)
        out_ref[held, :DH] = memory.astype(BF16)
        ones = jnp.ones((DK, 1), F32)
        parts = split3(normal)
        parts += split3(ones * jnp.maximum(total[h : h + 1], LOWEST))
        parts += split3(ones * peak[h : h + 1])
        out_ref[held, DH:] = place(parts, (DK, 128)).astype(BF16)


def combine_kernel(in_ref, *refs):
    out_ref = refs[-1]
    size = BLOCKS * SLICE
    tile = in_ref[:, DH:].astype(F32)
    across = tile.T
    decay = (across[3:4] + across[4:5]) + across[5:6]
    peak = (across[6:7] + across[7:8]) + across[8:9]
    shape = (BLOCKS, size)
    block, lane = rows(shape), lanes(shape)
    source = lax.shift_right_logical(lane, 3)
    earlier = source < block
    head_lane = (lane & (SLICE - 1)) == 0
    held = jnp.where(earlier & head_lane, decay, 0.0)
    total = jnp.sum(held, axis=1, keepdims=True)
    after = suffix_sum(jnp.where(lane < size - 1, pltpu.roll(held, size - 1, 1), 0.0))
    weight = peak + after
    running = jnp.maximum(
        total, jnp.max(jnp.where(earlier, weight, LOWEST), axis=1, keepdims=True)
    )
    factor = jnp.where(earlier, jnp.exp(jnp.minimum(weight - running, 0.0)), 0.0)
    spread = (
        lax.shift_right_logical(rows((size, BLOCKS)), 3) == lanes((size, BLOCKS))
    ).astype(BF16)
    same = (rows((size, size)) & (SLICE - 1)) == (lanes((size, size)) & (SLICE - 1))
    memory = jnp.zeros((size, DH), F32)
    scalars = jnp.zeros((size, 128), F32)
    for i, part in enumerate(split3(factor)):
        wide = jnp.dot(spread, part.astype(BF16), preferred_element_type=F32)
        wide = jnp.where(same, wide, 0.0).astype(BF16)
        scalars += jnp.dot(wide, in_ref[:, DH:], preferred_element_type=F32)
        if i < 2:
            memory += jnp.dot(wide, in_ref[:, :DH], preferred_element_type=F32)
    out_ref[:, :DH] = memory.astype(BF16)
    peaks = place(split3(running), (BLOCKS, 128)).astype(BF16)
    peaks = jnp.dot(spread, peaks, preferred_element_type=F32)
    normal = pick(scalars, 0, 3)
    entries = split3(normal) + split3(pick(peaks, 0, 3))
    out_ref[:, DH:] = place(entries, (size, 128)).astype(BF16)


def intra_kernel(q_hbm, k_hbm, v_hbm, ig_hbm, fg_hbm, _, numer_hbm, terms_hbm, *scratch):
    q_ref, k_ref, v_ref, ig_ref, fg_ref, numer_ref, terms_ref, sems = scratch
    copies = load(
        (
            (fg_hbm, fg_ref), (ig_hbm, ig_ref), (q_hbm, q_ref), (k_hbm, k_ref), (v_hbm, v_ref),
        ),
        sems,
    )
    for copy in copies[:2]:
        copy.wait()
    decay = decay_rows(fg_ref[...])
    offset = ig_ref[...]
    columns = to_columns(jnp.concatenate([decay, jnp.zeros((6, T), F32)], axis=0))
    causal = rows((T, T)) >= lanes((T, T))
    for copy in copies[2:]:
        copy.wait()
    terms = []
    stores = []
    for h in range(2):
        scores = (
            lax.dot_general(
                q_ref[:, h * DK : (h + 1) * DK],
                k_ref[:, h * DK : (h + 1) * DK],
                (((1,), (1,)), ((), ())),
                preferred_element_type=F32,
            )
            * SCALE
        )
        own = columns[:, h : h + 1]
        logits = own - decay[h : h + 1] + offset[h : h + 1]
        logits = jnp.where(causal, logits, -jnp.inf)
        row_peak = jnp.max(logits, axis=1, keepdims=True)
        weights = (jnp.exp(logits - row_peak) * scores).astype(BF16)
        held = numer_ref.at[:, h * DH : (h + 1) * DH]
        held[...] = jnp.dot(weights, v_ref[:, h * DH : (h + 1) * DH], preferred_element_type=F32)
        store = pltpu.make_async_copy(
            held, numer_hbm.at[:, h * DH : (h + 1) * DH], sems.at[5 + h]
        )
        store.start()
        stores.append(store)
        terms += [own, row_peak, jnp.sum(weights.astype(F32), axis=1, keepdims=True)]
    terms_ref[...] = place(terms, (T, 128))
    store = pltpu.make_async_copy(terms_ref, terms_hbm, sems.at[7])
    store.start()
    for store in stores + [store]:
        store.wait()


def readout_kernel(start, q_hbm, m_hbm, numer_hbm, terms_hbm, *refs):
    out_ref, q_ref, m_ref, numer_ref, terms_ref, sems = refs[-6:]
    mine = pl.ds(start, out_ref.shape[0])
    copies = load(
        (
            (m_hbm, m_ref), (q_hbm.at[mine], q_ref),
            (terms_hbm.at[mine], terms_ref), (numer_hbm.at[mine], numer_ref),
        ),
        sems,
    )
    for copy in copies:
        copy.wait()
    terms = terms_ref[...]
    for h in range(2):
        own, row_peak, denom = (terms[:, 3 * h + i : 3 * h + i + 1] for i in range(3))
        held = slice(h * DK, (h + 1) * DK)
        peak = pick(m_ref[h * DK : h * DK + 8, DH:].astype(F32), 3, 3)[:1]
        read = jnp.dot(q_ref[:, held], m_ref[held], preferred_element_type=F32) * SCALE
        prior = own + peak
        ceiling = jnp.maximum(prior, row_peak)
        prior_scale = jnp.exp(prior - ceiling)
        local_scale = jnp.exp(row_peak - ceiling)
        columns = slice(h * DH, (h + 1) * DH)
        numerator = prior_scale * read[:, :DH] + local_scale * numer_ref[:, columns]
        denominator = prior_scale * pick(read[:, DH:], 0, 3) + local_scale * denom
        floor_value = jnp.maximum(jnp.abs(denominator), 1.0)
        out_ref[:, columns] = (numerator / floor_value).astype(BF16)


def order_kernel(*refs):
    pass


def group_kernel(where_ref, *refs):
    pieces, out_ref = refs[:4], refs[-1]
    for i, piece in enumerate(pieces):
        slot = where_ref[2] ^ i
        out_ref[pl.ds(pl.multiple_of(slot * 64, 64), 64)] = piece[...]


def ring_kernel(where_ref, *refs):
    pieces, out_ref = refs[:4], refs[-1]
    start = jnp.where((where_ref[2] & 1) == 0, where_ref[1], where_ref[0])
    for r, piece in enumerate(pieces):
        out_ref[(start + r) & 3] = piece[...]


def product(first, where_ref, own_ref, other_ref, pieces, held, sems):
    x, y, c = where_ref[0], where_ref[1], where_ref[2] & 1
    blocks = (where_ref[first], where_ref[first + 1])

    def fetch(along_x, along_y):
        for s in range(2):
            for r in range(4):
                @pl.when(((x + r) & 3) == blocks[s])
                def _():
                    pltpu.make_async_copy(along_x[r], held.at[0, s], sems.at[s]).start()
        for s in range(2):
            for r in range(4):
                pltpu.make_async_copy(
                    along_y[r].at[blocks[s]], held.at[1, s, (y + r) & 3], sems.at[2 + s]
                ).start()

    @pl.when(c == 0)
    def _():
        fetch(pieces[:4], pieces[4:])

    @pl.when(c == 1)
    def _():
        fetch(pieces[4:], pieces[:4])

    total = jnp.zeros((own_ref.shape[0], 1024), F32)
    for half in range(2):
        for s, rows_ref in enumerate((own_ref, other_ref)):
            block = held.at[half, s]
            pltpu.make_async_copy(block, block, sems.at[2 * half + s]).wait()
            total += lax.dot_general(
                rows_ref[:, half * 512 : (half + 1) * 512],
                block[...].reshape(1024, 512),
                (((1,), (1,)), ((), ())),
                preferred_element_type=F32,
            )
    return total


def project_kernel(first, where_ref, own_ref, other_ref, *refs):
    out_ref, held, sems = refs[-3:]
    total = product(first, where_ref, own_ref, other_ref, refs[:8], held, sems)
    out_ref[...] = total.astype(out_ref.dtype)


def finish_kernel(start, where_ref, own_ref, other_ref, arrived_ref, *refs):
    out_hbm, held, sems, staged = refs[-4:]
    total = product(5, where_ref, own_ref, other_ref, refs[:8], held, sems)
    staged[...] = (total + arrived_ref[...].astype(F32)).astype(BF16)
    rows_out = out_hbm.at[pl.ds(start, staged.shape[0])]
    pltpu.async_copy(staged, rows_out, sems.at[0]).wait()


def add_kernel(start, kept_ref, arrived_ref, _, out_hbm, staged, sem):
    staged[...] = (kept_ref[...] + arrived_ref[...].astype(F32)).astype(BF16)
    pltpu.async_copy(staged, out_hbm.at[pl.ds(start, staged.shape[0])], sem).wait()


def call(kernel, out_shape, *operands, **kwargs):
    return pl.pallas_call(
        kernel,
        out_shape=out_shape,
        compiler_params=pltpu.CompilerParams(vmem_limit_bytes=16 * 1024 * 1024),
        **kwargs,
    )(*operands)


def shape(rows_, columns, dtype):
    return jax.ShapeDtypeStruct((rows_, columns), dtype)


SIZES = (4, 4, 2, 2, 4)
NAMES = SEQ + ("h",)
ANY = pl.BlockSpec(memory_space=pl.ANY)
VMEM = pl.BlockSpec(memory_space=pltpu.VMEM)
SMEM = pl.BlockSpec(memory_space=pltpu.SMEM)
HBM = pl.BlockSpec(memory_space=pltpu.MemorySpace.HBM)
SEM = pltpu.SemaphoreType.DMA


def fetch(a, source_of):
    places = [tuple(int(i) for i in p) for p in np.ndindex(*SIZES)]
    index = {p: i for i, p in enumerate(places)}
    return lax.ppermute(a, NAMES, [(index[source_of(*p)], index[p]) for p in places])


def paired(x, h):
    outer = h in (0, 3)
    moves = {1: 0, 2: 3} if outer else {0: 1, 3: 2}
    return (moves[x], h ^ 1) if x in moves else (x, h)


def along(turned, r):
    def source_of(x, y, z, c, h):
        if (c == 1) ^ turned:
            return ((x + r) % 4, y, z, c, h)
        return (x, (y + r) % 4, z, c, h)

    return source_of


def pinned(*arrays):
    return [pltpu.with_memory_space_constraint(a, pltpu.MemorySpace.HBM) for a in arrays]


def order(a, *after):
    return call(
        order_kernel, jax.ShapeDtypeStruct(a.shape, a.dtype), a, *after,
        in_specs=[ANY] * (1 + len(after)), out_specs=ANY, input_output_aliases={0: 0},
    )


def weight_near(out_weight):
    c = lax.axis_index("c")
    columns = out_weight.T
    low, high = columns[:, :512], columns[:, 512:]
    halves = (jnp.where(c == 0, low, high), jnp.where(c == 0, high, low))

    def source_of(dz, dc):
        def of(x, y, z, c, h):
            sx, sh = paired(x, h)
            return (sx, y, z ^ dz, c ^ dc, sh)

        return of

    return [fetch(halves[dc], source_of(dz, dc)) for dz in range(2) for dc in range(2)]


def per_device(queries, key_rows, value_rows, input_gate, forget_gate, out_weight):
    x, y, z, c, h = (lax.axis_index(n) for n in NAMES)
    outer = (h == 0) | (h == 3)
    keep = (h >= 2).astype(jnp.int32)

    def block(half, is_outer):
        return jnp.where(is_outer, 3 * half, 1 + half)

    where = jnp.stack(
        [
            x, y, 2 * z + c,
            block(1 - keep, outer), block(1 - keep, ~outer),
            block(keep, outer), block(keep, ~outer),
        ]
    ).astype(jnp.int32)

    near = weight_near(out_weight)
    gates = (input_gate.T, forget_gate.T)
    gate_space = [pltpu.VMEM((2, T), F32)] * 2
    summary = call(
        summary_kernel, shape(T, EXT, BF16), *pinned(key_rows, value_rows, *gates),
        in_specs=[HBM] * 4, out_specs=VMEM,
        scratch_shapes=[
            pltpu.VMEM((T, 2 * DK), BF16), pltpu.VMEM((T, 2 * DH), BF16), *gate_space, SEM((4,)),
        ],
    )
    grouped = lax.all_to_all(summary.reshape(BLOCKS, SLICE, EXT), SEQ, 0, 0, tiled=True)
    group = call(
        group_kernel, shape(256, 512, BF16), where, *near, summary,
        in_specs=[SMEM] + [VMEM] * 4 + [ANY], out_specs=VMEM,
    )
    ring = [group] + [fetch(group, along(False, r)) for r in (1, 2, 3)]
    plane = call(
        ring_kernel, jax.ShapeDtypeStruct((4, 256, 512), BF16), where, *ring,
        in_specs=[SMEM] + [VMEM] * 4, out_specs=VMEM,
    )
    pieces = [plane] + [fetch(plane, along(True, r)) for r in (1, 2, 3)]
    numer, terms = call(
        intra_kernel,
        (pltpu.MemorySpace.HBM((T, 2 * DH), F32), pltpu.MemorySpace.HBM((T, 128), F32)),
        *pinned(queries, key_rows, value_rows, *gates), near[3],
        in_specs=[HBM] * 5 + [ANY], out_specs=(HBM, HBM),
        scratch_shapes=[
            pltpu.VMEM((T, 2 * DK), BF16), pltpu.VMEM((T, 2 * DK), BF16),
            pltpu.VMEM((T, 2 * DH), BF16), *gate_space,
            pltpu.VMEM((T, 2 * DH), F32), pltpu.VMEM((T, 128), F32), SEM((8,)),
        ],
    )
    entering = call(
        combine_kernel, shape(T, EXT, BF16), grouped.reshape(T, EXT), plane, terms,
        in_specs=[VMEM, ANY, ANY], out_specs=VMEM,
    )
    carried = lax.all_to_all(entering.reshape(BLOCKS, SLICE, EXT), SEQ, 0, 0, tiled=True)
    carried = carried.reshape(T, EXT)

    starts = [sum(SIZES_OUT[:i]) for i in range(len(SIZES_OUT))]
    hiddens = []
    for start, size in zip(starts, SIZES_OUT):
        hiddens.append(call(
            functools.partial(readout_kernel, start), shape(size, 2 * DH, BF16),
            *pinned(queries, carried, numer, terms), *hiddens[-1:],
            in_specs=[HBM] * 4 + [ANY] * min(len(hiddens), 1), out_specs=VMEM,
            scratch_shapes=[
                pltpu.VMEM((size, 2 * DK), BF16), pltpu.VMEM((T, EXT), BF16),
                pltpu.VMEM((size, 2 * DH), F32), pltpu.VMEM((size, 128), F32), SEM((4,)),
            ],
        ))
    first = lax.ppermute(hiddens[0], "h", [(j, j ^ 1) for j in range(4)])
    pieces = [
        pieces[0], order(pieces[1], hiddens[-1]), order(pieces[2], first, hiddens[-1]),
        order(pieces[3], hiddens[-1]),
    ]
    pieces += [lax.ppermute(a, "c", [(0, 1), (1, 0)]) for a in pieces]
    held = [pltpu.VMEM((2, 2, 4, 256, 512), BF16), SEM((4,))]

    def project(first, dtype, hidden, other, *after):
        return call(
            functools.partial(project_kernel, first), shape(hidden.shape[0], 1024, dtype),
            where, hidden, other, *pieces, *after,
            in_specs=[SMEM, VMEM, VMEM] + [ANY] * (8 + len(after)), out_specs=VMEM,
            scratch_shapes=held,
        )

    out = None
    others, sends, arrivals = [], [], []
    for i, start in enumerate(starts):
        hidden = hiddens[i]
        other = first if i == 0 else lax.ppermute(hidden, "h", [(j, j ^ 1) for j in range(4)])
        others.append(other)
        after = []
        if i + 1 < len(hiddens):
            after = [other, *sends[max(i - 1, 0) : i]]
            hiddens[i + 1] = order(hiddens[i + 1], *after)
            after = hiddens[i + 1 : i + 2] if i == 0 else []
        send = project(3, BF16, hidden, other, *after)
        if i > 0:
            send = order(send, arrivals[i - 1])
        arrived = lax.ppermute(send, "h", [(j, 3 - j) for j in range(4)])
        sends.append(send)
        arrivals.append(arrived)
        before = [] if out is None else [out]
        staged = pltpu.VMEM((hidden.shape[0], 1024), BF16)
        if i < len(SIZES_OUT) - 1:
            out = call(
                functools.partial(finish_kernel, start), shape(T, 1024, BF16),
                where, hidden, other, arrived, *pieces, *before,
                in_specs=[SMEM, VMEM, VMEM, VMEM] + [ANY] * 8 + [HBM] * len(before),
                out_specs=HBM, scratch_shapes=held + [staged],
                input_output_aliases={12: 0} if before else {},
            )
        else:
            out = call(
                functools.partial(add_kernel, start), shape(T, 1024, BF16),
                project(5, F32, hidden, other), arrived, out,
                in_specs=[VMEM, VMEM, HBM], out_specs=HBM,
                scratch_shapes=[staged, SEM], input_output_aliases={2: 0},
            )
    return out


def solution(mesh):
    fine = Mesh(mesh.devices.reshape(4, 4, 2, 2, 4), SEQ + ("h",))
    both = P(SEQ, "h")
    return jax.shard_map(
        per_device,
        mesh=fine,
        in_specs=(both,) * 5 + (P("h", SEQ),),
        out_specs=both,
        check_vma=False,
    )
```
